128 devices in a mesh: seq: 32 (over y, x, core), tp: 4 (over z).
Axes of the slice: x: 4, y: 4, z: 4, core: 2. Of those that a mesh axis runs over, the one named last changes fastest.
Arguments:
- query_heads: bfloat16 [16384, 2048], P('seq', 'tp'), may hold values from -120 to 120
- key_heads: bfloat16 [16384, 2048], P('seq', 'tp'), may hold values from -120 to 120
- value_heads: bfloat16 [16384, 2048], P('seq', 'tp'), may hold values from -6 to 6
- out_weight: bfloat16 [2048, 2048], P('tp'), may hold values from -0.125 to 0.125
- cotangent: bfloat16 [16384, 2048], P('seq', 'tp'), may hold values from -6 to 6
- loss_mask: int32 [16384], P('seq'), may hold values 0 or 1
- block_pattern: int32 [64, 9], replicated, may hold values from 0 to 63, as said below
- block_counts: int32 [64], replicated, may hold values from 1 to 9
Outputs:
- attended: bfloat16 [16384, 2048], P('seq', 'tp')
- query_grad: bfloat16 [16384, 2048], P('seq', 'tp')
- key_grad: bfloat16 [16384, 2048], P('seq', 'tp')
- value_grad: bfloat16 [16384, 2048], P('seq', 'tp')
- weight_grad: float32 [2048, 2048], P('tp', 'seq')
The draws below stay inside these ranges and needn't reach their ends.
Inputs may be any that keep to these rules, and one draw needn't show every extreme that they name: For j < block_counts[b], block_pattern[b, j] are distinct blocks within 4 of b, the first being b itself; later entries are ignored.
All inputs are finite; a program needn't handle non-finite values. No bound on the sum of `loss_mask` on one device may be relied on, other than what follows from the above.
Results may differ from the reference program's by a relative error of at most 0.035.
Values may be sent and summed in bfloat16 or wider, within the bound.
No kernel may reach another device: no remote copies, remote signals or barrier semaphores. Data moves between devices by JAX's collectives and lax.ppermute only.
A program may use at most 192 MiB of HBM per device.

```python
import math
import jax
import jax.numpy as jnp
from jax import lax

D = 2048
HEADS = 16
HD = 128
BLK = 256
WINDOW = 4
LIST = 9
SEQ = 16384
NBLK = 64


def block_lists(shared_key):
    seed_order, seed_count = jax.random.split(jax.random.fold_in(shared_key, 11))
    offsets = jnp.concatenate([jnp.arange(-WINDOW, 0), jnp.arange(1, WINDOW + 1)]).astype(jnp.int32)
    query_ids = jnp.arange(NBLK, dtype=jnp.int32)[:, None]
    targets = query_ids + offsets[None, :]
    inside = (targets >= 0) & (targets < NBLK)
    ranks = jax.random.randint(seed_order, (NBLK, 2 * WINDOW), 0, 1 << 20) * (2 * WINDOW) + jnp.arange(2 * WINDOW, dtype=jnp.int32)[None, :]
    ranks = jnp.where(inside, ranks, ranks + (1 << 28))
    ordering = jnp.argsort(ranks, axis=1, stable=True)
    ordered = jnp.take_along_axis(targets, ordering, axis=1)
    ordered_in = jnp.take_along_axis(inside, ordering, axis=1)
    pattern = jnp.concatenate([query_ids, jnp.where(ordered_in, ordered, query_ids)], axis=1).astype(jnp.int32)
    available = 1 + jnp.sum(inside.astype(jnp.int32), axis=1)
    raw_count = jax.random.randint(seed_count, (NBLK,), 0, 1 << 20) % available
    counts = raw_count * raw_count // jnp.maximum(available - 1, 1) + 1
    counts = jnp.where(query_ids[:, 0] == WINDOW, available, counts).astype(jnp.int32)
    return (pattern, counts)


def draw_block_pattern(key, part):
    shared = block_lists(key)
    return shared[0]


def draw_block_counts(key, part):
    shared = block_lists(key)
    return shared[1]


def draw_query_heads(key, part):
    key = jax.random.fold_in(key, 5)
    values = jnp.clip(jax.random.normal(key, (SEQ, D), jnp.float32), -6.0, 6.0)
    return values.astype(jnp.bfloat16)


def draw_key_heads(key, part):
    key = jax.random.fold_in(key, 6)
    values = jnp.clip(jax.random.normal(key, (SEQ, D), jnp.float32), -6.0, 6.0)
    return values.astype(jnp.bfloat16)


def set_ends(values, own_key, least, largest):
    index_at = [jax.random.randint(jax.random.fold_in(own_key, axis), (), 0, length) for axis, length in enumerate(values.shape)]
    main_axis = values.shape.index(max(values.shape))
    beside = index_at[:main_axis] + [(index_at[main_axis] + 1) % values.shape[main_axis]] + index_at[main_axis + 1:]
    return values.at[tuple(index_at)].set(least).at[tuple(beside)].set(largest)


def block_levels(key, dims, pieces, low, largest):
    gain = 1.0
    for dim, blocks in pieces:
        steps = jax.random.uniform(jax.random.fold_in(jax.random.fold_in(key, 6), dim), (blocks,), jnp.float32, low / len(pieces), largest / len(pieces))
        gain = gain * jnp.repeat(jnp.exp(steps), dims[dim] // blocks).reshape((-1,) + (1,) * (len(dims) - 1 - dim))
    return gain


def gaussian(rng, shape, scale, reach, cuts=(), held_as=jnp.bfloat16):
    array = scale * jax.random.normal(rng, shape, jnp.float32)
    if cuts:
        array = array * block_levels(rng, shape, cuts, -0.22, 0.18)
    return jnp.clip(array, -reach, reach).astype(held_as)


def setup_inputs(seed: int = 0) -> dict:
    streams_of = jax.random.split(jax.random.key(seed), 9)
    return {
        "query_heads": draw_query_heads(jax.random.fold_in(streams_of[8], 71), 0),
        "key_heads": draw_key_heads(jax.random.fold_in(streams_of[8], 71), 0),
        "value_heads": gaussian(streams_of[2], (SEQ, HEADS * HD), 1.0, 6.0, ((0, 32), (1, 4))),
        "out_weight": gaussian(streams_of[3], (HEADS * HD, D), (HEADS * HD) ** -0.5, 0.125, ((0, 4),)),
        "cotangent": gaussian(streams_of[4], (SEQ, D), 1.0, 6.0, ((0, 32), (1, 4))),
        "loss_mask": set_ends((jax.random.randint(streams_of[5], (SEQ,), 0, 2) < 1).astype(jnp.int32), jax.random.fold_in(streams_of[5], 1), 0, 1),
        "block_pattern": draw_block_pattern(jax.random.fold_in(streams_of[8], 71), 0),
        "block_counts": draw_block_counts(jax.random.fold_in(streams_of[8], 71), 0),
    }


def take_blocks(source, block_ids):

    def one_block(block_id):
        return lax.dynamic_slice_in_dim(source, (block_id * BLK).astype(jnp.int32), BLK, 0)
    return jax.vmap(one_block)(block_ids).reshape(LIST, BLK, HEADS, HD).astype(jnp.float32)

def block_scores(query_block, key_blocks, listed):
    logits = jnp.einsum('qhd,lkhd->hqlk', query_block, key_blocks) * (1.0 / math.sqrt(HD))
    return jnp.where(listed[None, None, :, None], logits, -jnp.inf)

def reference(query_heads, key_heads, value_heads, out_weight, cotangent, loss_mask, block_pattern, block_counts):
    slot_live = jnp.arange(LIST, dtype=jnp.int32)[None, :] < block_counts[:, None]
    block_range = jnp.arange(NBLK, dtype=jnp.int32)

    def forward_block(block_id):
        block_ids = block_pattern[block_id]
        listed = slot_live[block_id]
        row_start = (block_id * BLK).astype(jnp.int32)
        query_block = lax.dynamic_slice_in_dim(query_heads, row_start, BLK, 0).reshape(BLK, HEADS, HD).astype(jnp.float32)
        logits = block_scores(query_block, take_blocks(key_heads, block_ids), listed)
        highest = lax.optimization_barrier(jnp.max(logits, axis=(2, 3), keepdims=True))
        log_total = highest + jnp.log(lax.optimization_barrier(jnp.sum(jnp.exp(logits - highest), axis=(2, 3), keepdims=True)))
        weights = lax.optimization_barrier(jnp.exp(logits - log_total).astype(jnp.bfloat16)).astype(jnp.float32)
        blended = jnp.einsum('hqlk,lkhd->qhd', weights, take_blocks(value_heads, block_ids))
        return (blended.reshape(BLK, HEADS * HD).astype(jnp.bfloat16), log_total[:, :, 0, 0])
    heads_out, log_totals = lax.map(forward_block, block_range)
    heads_out = heads_out.reshape(SEQ, HEADS * HD)
    attended = jnp.dot(heads_out, out_weight, preferred_element_type=jnp.float32).astype(jnp.bfloat16)
    masked = jnp.where(loss_mask[:, None] == 1, cotangent, jnp.zeros_like(cotangent))
    weight_grad = jnp.dot(heads_out.T, masked, preferred_element_type=jnp.float32)
    d_heads = jnp.dot(masked, out_weight.T, preferred_element_type=jnp.float32).astype(jnp.bfloat16)
    row_dots = lax.optimization_barrier(jnp.sum((d_heads.astype(jnp.float32) * heads_out.astype(jnp.float32)).reshape(SEQ, HEADS, HD), axis=2))

    def backward_block(carried, block_id):
        key_acc, value_acc = carried
        block_ids = block_pattern[block_id]
        listed = slot_live[block_id]
        row_start = (block_id * BLK).astype(jnp.int32)
        query_block = lax.dynamic_slice_in_dim(query_heads, row_start, BLK, 0).reshape(BLK, HEADS, HD).astype(jnp.float32)
        grad_block = lax.dynamic_slice_in_dim(d_heads, row_start, BLK, 0).reshape(BLK, HEADS, HD).astype(jnp.float32)
        dots_block = lax.dynamic_slice_in_dim(row_dots, row_start, BLK, 0).T
        key_blocks = take_blocks(key_heads, block_ids)
        value_blocks = take_blocks(value_heads, block_ids)
        logits = block_scores(query_block, key_blocks, listed)
        weights = jnp.exp(logits - log_totals[block_id][:, :, None, None])
        weights_b = lax.optimization_barrier(weights.astype(jnp.bfloat16)).astype(jnp.float32)
        d_probs = jnp.einsum('qhd,lkhd->hqlk', grad_block, value_blocks)
        d_logits = weights * (d_probs - dots_block[:, :, None, None]) * (1.0 / math.sqrt(HD))
        d_logits = lax.optimization_barrier(d_logits.astype(jnp.bfloat16)).astype(jnp.float32)
        query_grad = jnp.einsum('hqlk,lkhd->qhd', d_logits, key_blocks).reshape(BLK, HEADS * HD).astype(jnp.bfloat16)
        key_parts = jnp.einsum('hqlk,qhd->lkhd', d_logits, query_block).reshape(LIST, BLK, HEADS * HD)
        value_parts = jnp.einsum('hqlk,qhd->lkhd', weights_b, grad_block).reshape(LIST, BLK, HEADS * HD)
        for slot_id in range(LIST):
            block_row = (block_ids[slot_id] * BLK).astype(jnp.int32)
            key_acc = lax.dynamic_update_slice_in_dim(key_acc, lax.dynamic_slice_in_dim(key_acc, block_row, BLK, 0) + key_parts[slot_id], block_row, 0)
            value_acc = lax.dynamic_update_slice_in_dim(value_acc, lax.dynamic_slice_in_dim(value_acc, block_row, BLK, 0) + value_parts[slot_id], block_row, 0)
        return ((key_acc, value_acc), query_grad)
    zero_acc = jnp.zeros((SEQ, HEADS * HD), jnp.float32)
    (key_acc, value_acc), query_grads = lax.scan(backward_block, (zero_acc, zero_acc), block_range)
    query_grad = query_grads.reshape(SEQ, HEADS * HD)
    return (attended, query_grad, key_acc.astype(jnp.bfloat16), value_acc.astype(jnp.bfloat16), weight_grad)
```

```python
import math

import jax
import jax.numpy as jnp
from jax import lax
from jax.experimental import pallas as pl
from jax.experimental.pallas import tpu as pltpu
from jax.sharding import PartitionSpec as P

HD = 128
BLK = 256
WINDOW = 4
SCALE = 1.0 / math.sqrt(HD)
TWO = SCALE * math.log2(math.e)
STAT_ROWS = 32
VMEM_LIMIT = 40 * 1024 * 1024

NT = (((1,), (1,)), ((), ()))
NN = (((1,), (0,)), ((), ()))
TN = (((0,), (0,)), ((), ()))


def mm(a, b, dims):
    return lax.dot_general(a, b, dims, preferred_element_type=jnp.float32)


def shifted(value, steps):
    count = lax.axis_size("seq")
    pairs = [(i, i + steps) for i in range(count) if 0 <= i + steps < count]
    return lax.ppermute(value, "seq", pairs)


def swapped(value):
    return lax.ppermute(value, "seq", [(i, i ^ 1) for i in range(lax.axis_size("seq"))])


def relayed(from_left, from_right):
    count = lax.axis_size("seq")
    to_even = lax.ppermute(from_left, "seq", [(i, i - 1) for i in range(1, count, 2)])
    to_odd = lax.ppermute(from_right, "seq", [(i, i + 1) for i in range(0, count, 2)])
    return to_even, to_odd


def start_halo(core, refs, buf, sems, first, with_own):
    own, mate, left, right, to_even, to_odd = refs
    rows = left.shape[0]

    def slot(index):
        return buf.at[pl.ds(pl.multiple_of(index * rows, 32), rows)]

    copies = [
        pltpu.make_async_copy(left, slot(0), sems.at[first]),
        pltpu.make_async_copy(right, slot(4), sems.at[first + 1]),
        pltpu.make_async_copy(mate, slot(3 - 2 * core), sems.at[first + 2]),
    ]
    if with_own:
        copies.append(pltpu.make_async_copy(own, slot(2), sems.at[first + 3]))
    for copy in copies:
        copy.start()
    even = pltpu.make_async_copy(to_even, slot(1), sems.at[first + 4])
    odd = pltpu.make_async_copy(to_odd, slot(3), sems.at[first + 4])

    @pl.when(core == 0)
    def _():
        even.start()

    @pl.when(core != 0)
    def _():
        odd.start()

    return copies + [even]


def forward_kernel(pos_ref, pat_ref, cnt_ref, q_ref, mask_ref, *rest):
    k_refs, v_refs = rest[:6], rest[6:12]
    out_ref, masked_t_ref, lse_ref, kbuf, vbuf, acc, sems = rest[12:]
    pos = pos_ref[0]
    core = pos % 2
    rows, cols = q_ref.shape
    heads, blocks = cols // HD, rows // BLK
    waits = start_halo(core, k_refs, kbuf, sems, 0, True)
    waits += start_halo(core, v_refs, vbuf, sems, 5, True)
    for copy in waits:
        copy.wait()
    for i in range(blocks):
        block = pos * blocks + i
        tok = slice(i * BLK, (i + 1) * BLK)
        acc[...] = jnp.zeros_like(acc)

        def body(j, carry):
            row = pl.multiple_of((pat_ref[block, j] - pos * blocks + WINDOW) * BLK, BLK)
            after = []
            for h in range(heads):
                col = slice(h * HD, (h + 1) * HD)
                top, total = carry[h]
                s = mm(kbuf[pl.ds(row, BLK), col], q_ref[tok, col], NT)
                new_top = jnp.maximum(top, jnp.max(s, axis=0, keepdims=True))
                p = jnp.exp2(s * TWO - new_top * TWO)
                fade = jnp.exp2((top - new_top) * TWO)
                total = total * fade + jnp.sum(p, axis=0, keepdims=True)
                acc[h] = acc[h] * fade + mm(
                    vbuf[pl.ds(row, BLK), col], p.astype(jnp.bfloat16), TN
                )
                after.append((new_top, total))
            return tuple(after)

        low = jnp.full((1, BLK), -1e30, jnp.float32)
        none = jnp.zeros((1, BLK), jnp.float32)
        ends = lax.fori_loop(0, cnt_ref[block], body, ((low, none),) * heads)
        for h in range(heads):
            col = slice(h * HD, (h + 1) * HD)
            top, total = ends[h]
            out_t = acc[h] * (1.0 / total)
            out_ref[tok, col] = out_t.T.astype(jnp.bfloat16)
            masked_t_ref[col, tok] = jnp.where(mask_ref[:, tok] == 1, out_t, 0.0).astype(
                jnp.bfloat16
            )
            lse_ref[h : h + 1, tok] = top * TWO + jnp.log(total) * math.log2(math.e)


def heads_grad_kernel(cot_ref, weight_ref, mask_ref, out_ref, lse_ref, sent_ref, dots):
    step = pl.program_id(0)
    rows = cot_ref.shape[0]
    half = weight_ref.shape[0]
    grad = mm(cot_ref[...], weight_ref[...], NT)
    grad = jnp.where(mask_ref[...] == 1, grad, 0.0).astype(jnp.bfloat16)
    col = pl.ds(pl.multiple_of(step * half, HD), half)
    sent_ref[0:rows, col] = grad
    products = grad.astype(jnp.float32) * out_ref[:, col].astype(jnp.float32)
    for h in range(half // HD):
        dots[pl.ds(step * (half // HD) + h, 1), :] = jnp.sum(
            products[:, h * HD : (h + 1) * HD].T, axis=0, keepdims=True
        )

    @pl.when(step == pl.num_programs(0) - 1)
    def _():
        stats = jnp.concatenate([lse_ref[...], dots[...]], axis=0)
        high = stats.astype(jnp.bfloat16).astype(jnp.float32)
        middle = (stats - high).astype(jnp.bfloat16).astype(jnp.float32)
        low = stats - high - middle
        parts = jnp.concatenate([high, middle, low, jnp.zeros_like(low)], axis=0)
        sent_ref[rows : rows + STAT_ROWS, :] = parts.astype(jnp.bfloat16)


def joined_stats(parts):
    parts = parts.astype(jnp.float32)
    return parts[0:8] + parts[8:16] + parts[16:24]


def query_grad_kernel(pos_ref, pat_ref, cnt_ref, q_ref, g_ref, *rest):
    k_refs, v_refs = rest[:6], rest[6:12]
    dq_ref, dk_ref, dv_ref, kbuf, vbuf, acc, sems = rest[12:]
    pos = pos_ref[0]
    core = pos % 2
    rows, cols = q_ref.shape
    heads, blocks = cols // HD, rows // BLK
    waits = start_halo(core, k_refs, kbuf, sems, 0, True)
    waits += start_halo(core, v_refs, vbuf, sems, 5, True)
    dk_ref[...] = jnp.zeros_like(dk_ref)
    dv_ref[...] = jnp.zeros_like(dv_ref)
    stats = joined_stats(g_ref[rows : rows + STAT_ROWS, :])
    for copy in waits:
        copy.wait()
    for i in range(blocks):
        block = pos * blocks + i
        tok = slice(i * BLK, (i + 1) * BLK)
        acc[...] = jnp.zeros_like(acc)

        def body(j, carry):
            place = pat_ref[block, j] - pos * blocks
            row = pl.multiple_of((place + WINDOW) * BLK, BLK)
            kept = []
            for h in range(heads):
                col = slice(h * HD, (h + 1) * HD)
                lse = stats[h : h + 1, tok]
                dots = stats[heads + h : heads + h + 1, tok]
                k = kbuf[pl.ds(row, BLK), col]
                s = mm(k, q_ref[tok, col], NT)
                p = jnp.exp2(s * TWO - lse)
                dp = mm(vbuf[pl.ds(row, BLK), col], g_ref[tok, col], NT)
                ds = (p * (dp - dots)).astype(jnp.bfloat16)
                acc[h] += mm(k, ds, TN)
                kept.append((p.astype(jnp.bfloat16), ds))

            @pl.when((place >= 0) & (place < blocks))
            def _():
                own = pl.ds(pl.multiple_of(place * BLK, BLK), BLK)
                for h in range(heads):
                    col = slice(h * HD, (h + 1) * HD)
                    p, ds = kept[h]
                    dv_ref[own, col] += mm(p, g_ref[tok, col], NN)
                    dk_ref[own, col] += mm(ds, q_ref[tok, col], NN)

            return carry

        lax.fori_loop(0, cnt_ref[block], body, 0)
        for h in range(heads):
            col = slice(h * HD, (h + 1) * HD)
            dq_ref[tok, col] = (acc[h] * SCALE).T.astype(jnp.bfloat16)


def key_grad_kernel(pos_ref, pat_ref, cnt_ref, k_ref, v_ref, dk_in, dv_in, *rest):
    q_refs, g_refs = rest[:5], rest[5:10]
    dk_ref, dv_ref, qbuf, gbuf, dk, dv, sems = rest[10:]
    pos = pos_ref[0]
    core = pos % 2
    rows, cols = k_ref.shape
    heads, blocks = cols // HD, rows // BLK
    all_blocks = pat_ref.shape[0]
    sent_rows = rows + STAT_ROWS
    waits = start_halo(core, (None,) + tuple(q_refs), qbuf, sems, 0, False)
    waits += start_halo(core, (None,) + tuple(g_refs), gbuf, sems, 5, False)
    dk[...] = dk_in[...]
    dv[...] = dv_in[...]
    for copy in waits:
        copy.wait()

    def from_block(t, carry):
        near = jnp.where(t >= WINDOW, t + blocks, t)
        block = pos * blocks - WINDOW + near
        inside = (block >= 0) & (block < all_blocks)
        block = jnp.clip(block, 0, all_blocks - 1)
        device, part = near // blocks, near % blocks
        q_row = pl.multiple_of(near * BLK, BLK)
        g_base = device * sent_rows
        g_row = pl.multiple_of(g_base + part * BLK, 32)
        stats = joined_stats(gbuf[pl.ds(pl.multiple_of(g_base + rows, 32), STAT_ROWS), :])
        chosen = stats[:, 0:BLK]
        for other in range(1, blocks):
            chosen = jnp.where(part == other, stats[:, other * BLK : (other + 1) * BLK], chosen)

        def body(j, carry):
            place = pat_ref[block, j] - pos * blocks

            @pl.when((place >= 0) & (place < blocks))
            def _():
                own = pl.ds(pl.multiple_of(place * BLK, BLK), BLK)
                for h in range(heads):
                    col = slice(h * HD, (h + 1) * HD)
                    q = qbuf[pl.ds(q_row, BLK), col]
                    g = gbuf[pl.ds(g_row, BLK), col]
                    s = mm(k_ref[own, col], q, NT)
                    p = jnp.exp2(s * TWO - chosen[h : h + 1])
                    dp = mm(v_ref[own, col], g, NT)
                    ds = (p * (dp - chosen[heads + h : heads + h + 1])).astype(jnp.bfloat16)
                    dv[own, col] += mm(p.astype(jnp.bfloat16), g, NN)
                    dk[own, col] += mm(ds, q, NN)

            return carry

        lax.fori_loop(0, jnp.where(inside, cnt_ref[block], 0), body, 0)
        return carry

    lax.fori_loop(0, 2 * WINDOW, from_block, 0)
    dk_ref[...] = (dk[...] * SCALE).astype(jnp.bfloat16)
    dv_ref[...] = dv[...].astype(jnp.bfloat16)


SMEM = pl.BlockSpec(memory_space=pltpu.SMEM)
VMEM = pl.BlockSpec(memory_space=pltpu.VMEM)
ANY = pl.BlockSpec(memory_space=pl.ANY)
PARAMS = pltpu.CompilerParams(vmem_limit_bytes=VMEM_LIMIT)


def shape(dims, dtype=jnp.bfloat16):
    return jax.ShapeDtypeStruct(dims, dtype)


def local(
    query_heads,
    key_heads,
    value_heads,
    out_weight,
    cotangent,
    loss_mask,
    block_pattern,
    block_counts,
):
    rows, cols = query_heads.shape
    heads = cols // HD
    width = out_weight.shape[1]
    position = lax.axis_index("seq")
    core = position % 2
    where = jnp.reshape(position, (1,)).astype(jnp.int32)
    tables = (where, block_pattern, block_counts)

    full_cot = lax.all_gather(cotangent, "tp", axis=1, tiled=True)

    key_mate, value_mate, query_mate = (swapped(x) for x in (key_heads, value_heads, query_heads))
    key_left, key_right = shifted(key_heads, 2), shifted(key_heads, -2)
    value_left, value_right = shifted(value_heads, 2), shifted(value_heads, -2)
    keys = (key_heads, key_mate, key_left, key_right) + relayed(key_left, key_right)
    values = (value_heads, value_mate, value_left, value_right) + relayed(value_left, value_right)
    query_after, _, _ = lax.optimization_barrier((query_heads, value_left, value_right))
    query_left, query_right = shifted(query_after, 2), shifted(query_after, -2)
    queries = (query_mate, query_left, query_right) + relayed(query_left, query_right)

    halo = 5 * rows
    heads_out, masked_t, log_total = pl.pallas_call(
        forward_kernel,
        out_shape=(shape((rows, cols)), shape((cols, rows)), shape((heads, rows), jnp.float32)),
        in_specs=[SMEM] * 3 + [VMEM] * 2 + [ANY] * 12,
        out_specs=(VMEM,) * 3,
        scratch_shapes=[
            pltpu.VMEM((halo, cols), jnp.bfloat16),
            pltpu.VMEM((halo, cols), jnp.bfloat16),
            pltpu.VMEM((heads, HD, BLK), jnp.float32),
            pltpu.SemaphoreType.DMA((10,)),
        ],
        compiler_params=PARAMS,
        name="attention_forward",
    )(*tables, query_heads, loss_mask.reshape(1, rows), *keys, *values)

    partial_out = jnp.dot(heads_out, out_weight, preferred_element_type=jnp.float32)
    attended = lax.psum_scatter(
        partial_out.astype(jnp.bfloat16), "tp", scatter_dimension=1, tiled=True
    )

    steps = 2
    sent = pl.pallas_call(
        heads_grad_kernel,
        grid=(steps,),
        out_shape=shape((rows + STAT_ROWS, cols)),
        in_specs=[
            pl.BlockSpec((rows, width), lambda i: (0, 0)),
            pl.BlockSpec((cols // steps, width), lambda i: (i, 0)),
            pl.BlockSpec((rows, 1), lambda i: (0, 0)),
            pl.BlockSpec((rows, cols), lambda i: (0, 0)),
            pl.BlockSpec((heads, rows), lambda i: (0, 0)),
        ],
        out_specs=pl.BlockSpec((rows + STAT_ROWS, cols), lambda i: (0, 0)),
        scratch_shapes=[pltpu.VMEM((heads, rows), jnp.float32)],
        compiler_params=PARAMS,
        name="heads_grad",
    )(full_cot, out_weight, loss_mask.reshape(rows, 1), heads_out, log_total)

    sent_mate = swapped(sent)
    sent_left, sent_right = shifted(sent, 2), shifted(sent, -2)
    grads = (sent_mate, sent_left, sent_right) + relayed(sent_left, sent_right)

    query_grad, key_own, value_own = pl.pallas_call(
        query_grad_kernel,
        out_shape=(
            shape((rows, cols)),
            shape((rows, cols), jnp.float32),
            shape((rows, cols), jnp.float32),
        ),
        in_specs=[SMEM] * 3 + [VMEM] * 2 + [ANY] * 12,
        out_specs=(VMEM,) * 3,
        scratch_shapes=[
            pltpu.VMEM((halo, cols), jnp.bfloat16),
            pltpu.VMEM((halo, cols), jnp.bfloat16),
            pltpu.VMEM((heads, HD, BLK), jnp.float32),
            pltpu.SemaphoreType.DMA((10,)),
        ],
        compiler_params=PARAMS,
        name="query_grad",
    )(*tables, query_heads, sent, *keys, *values)

    chips = lax.axis_size("seq") // 2
    part = jnp.dot(masked_t, full_cot, preferred_element_type=jnp.float32).astype(jnp.bfloat16)
    part = part.reshape(2, cols // 2, chips, width // chips).transpose(0, 2, 1, 3)
    mine = lax.dynamic_index_in_dim(part, core, 0, keepdims=False)
    theirs = lax.dynamic_index_in_dim(part, 1 - core, 0, keepdims=False)
    arrived = swapped(theirs)
    chip_sum = (mine.astype(jnp.float32) + arrived.astype(jnp.float32)).astype(jnp.bfloat16)
    same_core = [[2 * i + c for i in range(chips)] for c in range(2)]
    spread = lax.all_to_all(chip_sum, "seq", 0, 0, axis_index_groups=same_core, tiled=True)
    summed = jnp.sum(spread.astype(jnp.float32), axis=0)
    narrow = width // chips // 2
    keep = lax.dynamic_slice_in_dim(summed, core * narrow, narrow, 1)
    give = lax.dynamic_slice_in_dim(summed, (1 - core) * narrow, narrow, 1)
    got = swapped(give)
    weight_grad = jnp.where(
        core == 0, jnp.concatenate([keep, got], 0), jnp.concatenate([got, keep], 0)
    )

    key_grad, value_grad = pl.pallas_call(
        key_grad_kernel,
        out_shape=(shape((rows, cols)), shape((rows, cols))),
        in_specs=[SMEM] * 3 + [VMEM] * 4 + [ANY] * 10,
        out_specs=(VMEM,) * 2,
        scratch_shapes=[
            pltpu.VMEM((halo, cols), jnp.bfloat16),
            pltpu.VMEM((halo + 5 * STAT_ROWS, cols), jnp.bfloat16),
            pltpu.VMEM((rows, cols), jnp.float32),
            pltpu.VMEM((rows, cols), jnp.float32),
            pltpu.SemaphoreType.DMA((10,)),
        ],
        compiler_params=PARAMS,
        name="key_grad",
    )(*tables, key_heads, value_heads, key_own, value_own, *queries, *grads)
    return (attended, query_grad, key_grad, value_grad, weight_grad)


def solution(mesh):
    in_specs = (
        P("seq", "tp"),
        P("seq", "tp"),
        P("seq", "tp"),
        P("tp", None),
        P("seq", "tp"),
        P("seq"),
        P(),
        P(),
    )
    out_specs = (P("seq", "tp"), P("seq", "tp"), P("seq", "tp"), P("seq", "tp"), P("tp", "seq"))
    return jax.shard_map(local, mesh=mesh, in_specs=in_specs, out_specs=out_specs, check_vma=False)
```

```python
import math

import jax
import jax.numpy as jnp
from jax import lax
from jax.experimental import pallas as pl
from jax.experimental.pallas import tpu as pltpu
from jax.sharding import PartitionSpec as P

HD = 128
BLK = 256
WINDOW = 4
SCALE = 1.0 / math.sqrt(HD)
TWO = SCALE * math.log2(math.e)
STAT_ROWS = 32
CHUNK = 4
SHIFTS = (0, 3, 1, 2, 2)

NT = (((1,), (1,)), ((), ()))
NN = (((1,), (0,)), ((), ()))
TN = (((0,), (0,)), ((), ()))


def mm(a, b, dims):
    return lax.dot_general(a, b, dims, preferred_element_type=jnp.float32)


def shifted(value, steps):
    count = lax.axis_size("seq")
    return lax.ppermute(value, "seq", [(i, (i + steps) % count) for i in range(count)])


def swapped(value):
    return lax.ppermute(value, "seq", [(i, i ^ 1) for i in range(lax.axis_size("seq"))])


def along_tp(value, steps):
    count = lax.axis_size("tp")
    return lax.ppermute(value, "tp", [(i, (i + steps) % count) for i in range(count)])


def relayed(from_left, from_right):
    return swapped(from_left), swapped(from_right)


def start_halo(core, refs, buf, sems, first, with_own):
    own, mate, left, right, to_even, to_odd = refs
    rows = left.shape[0]

    def slot(index):
        return buf.at[pl.ds(pl.multiple_of(index * rows, 32), rows)]

    copies = [
        pltpu.make_async_copy(left, slot(0), sems.at[first]),
        pltpu.make_async_copy(right, slot(4), sems.at[first + 1]),
        pltpu.make_async_copy(mate, slot(3 - 2 * core), sems.at[first + 2]),
    ]
    if with_own:
        copies.append(pltpu.make_async_copy(own, slot(2), sems.at[first + 3]))
    for copy in copies:
        copy.start()
    even = pltpu.make_async_copy(to_even, slot(1), sems.at[first + 4])
    odd = pltpu.make_async_copy(to_odd, slot(3), sems.at[first + 4])

    @pl.when(core == 0)
    def _():
        even.start()

    @pl.when(core != 0)
    def _():
        odd.start()

    return copies + [even]


def in_chunks(count, body):
    def whole(c, carry):
        body(c * CHUNK, CHUNK)
        return carry

    lax.fori_loop(0, count // CHUNK, whole, 0)
    rest = count % CHUNK
    for size in range(1, CHUNK):

        @pl.when(rest == size)
        def _():
            body(count - size, size)


def stacked(ref, rows, col):
    return jnp.concatenate([ref[pl.ds(row, BLK), col] for row in rows], axis=0)


def folded(x, op):
    total = x[:, :HD]
    for i in range(1, x.shape[1] // HD):
        total = op(total, x[:, i * HD : (i + 1) * HD])
    return total


def forward_kernel(pos_ref, pat_ref, cnt_ref, q_ref, mask_ref, weight_hbm, *rest):
    pieces, rest = rest[:5], rest[5:]
    k_refs, v_refs = rest[:6], rest[6:12]
    out_ref, masked_t_ref, sent_ref, kbuf, vbuf, wbuf, cbuf, top, total, acc, stats, sems = rest[12:]
    pos = pos_ref[0]
    core = pos % 2
    rows, cols = q_ref.shape
    heads, blocks = cols // HD, rows // BLK
    waits = start_halo(core, k_refs, kbuf, sems, 0, True)
    waits += start_halo(core, v_refs, vbuf, sems, 5, True)
    ranks = wbuf.shape[1] // cols
    later = [pltpu.make_async_copy(weight_hbm, wbuf, sems.at[10])]
    for x, (piece, shift) in enumerate(zip(pieces, SHIFTS)):
        low = 0 if x < ranks else rows - piece.shape[0]
        place = cbuf.at[
            pl.ds(low, piece.shape[0]),
            pl.ds(pl.multiple_of((pos_ref[1] + shift) % ranks * cols, HD), cols),
        ]
        later.append(pltpu.make_async_copy(piece, place, sems.at[11 + x]))
    for copy in later:
        copy.start()
    for copy in waits:
        copy.wait()
    for i in range(blocks):
        block = pos * blocks + i
        tok = slice(i * BLK, (i + 1) * BLK)
        top[...] = jnp.full_like(top, -1e30)
        total[...] = jnp.zeros_like(total)
        acc[...] = jnp.zeros_like(acc)

        def body(first, size):
            places = [
                pl.multiple_of((pat_ref[first + c, block] - pos * blocks + WINDOW) * BLK, BLK)
                for c in range(size)
            ]
            for h in range(heads):
                col = slice(h * HD, (h + 1) * HD)
                s = mm(q_ref[tok, col], stacked(kbuf, places, col), NT)
                high = jnp.max(folded(s, jnp.maximum), axis=1, keepdims=True) * TWO
                old = top[h]
                new = jnp.maximum(old, high)
                p = jnp.exp2(s * TWO - jnp.concatenate([new] * (2 * size), 1))
                fade = jnp.exp2(old - new)
                top[h] = new
                total[h] = total[h] * fade + folded(p, jnp.add)
                acc[h] = acc[h] * fade + mm(
                    p.astype(jnp.bfloat16), stacked(vbuf, places, col), NN
                )

        in_chunks(cnt_ref[block], body)
        for h in range(heads):
            col = slice(h * HD, (h + 1) * HD)
            whole = jnp.sum(total[h], axis=1, keepdims=True)
            out = acc[h] * (1.0 / whole)
            rounded = out.astype(jnp.bfloat16)
            out_ref[tok, col] = rounded
            masked_t_ref[col, tok] = jnp.where(mask_ref[:, tok] == 1, out.T, 0.0).astype(
                jnp.bfloat16
            )
            lse = top[h] + jnp.log(whole) * math.log2(math.e)
            stats[h : h + 1, tok] = lse.T[0:1]
    for copy in later:
        copy.wait()
    kept = jnp.broadcast_to(mask_ref[...], (HD, rows)).astype(jnp.float32).T == 1.0
    half = cols // 2
    for part in range(2):
        grad = mm(cbuf[...], wbuf[part * half : (part + 1) * half, :], NT)
        for h in range(half // HD):
            head = part * (half // HD) + h
            col = slice(head * HD, (head + 1) * HD)
            one = jnp.where(kept, grad[:, h * HD : (h + 1) * HD], 0.0).astype(jnp.bfloat16)
            sent_ref[0:rows, col] = one
            dots = one.astype(jnp.float32) * out_ref[:, col].astype(jnp.float32)
            stats[heads + head : heads + head + 1, :] = jnp.sum(dots.T, axis=0, keepdims=True)
    whole = stats[...]
    high = whole.astype(jnp.bfloat16).astype(jnp.float32)
    middle = (whole - high).astype(jnp.bfloat16).astype(jnp.float32)
    low = whole - high - middle
    parts = jnp.concatenate([high, middle, low, jnp.zeros_like(low)], axis=0)
    sent_ref[rows : rows + STAT_ROWS, :] = parts.astype(jnp.bfloat16)


def project_kernel(where_ref, out_ref, weight_hbm, own_ref, *rest):
    sends, (wbuf, sems) = rest[:-2], rest[-2:]
    ranks, cols = wbuf.shape[0], own_ref.shape[1]
    copies = []
    for shift in range(ranks):
        first = pl.multiple_of((where_ref[1] + shift) % ranks * cols, HD)
        copies.append(
            pltpu.make_async_copy(
                weight_hbm.at[:, pl.ds(first, cols)], wbuf.at[shift], sems.at[shift]
            )
        )
        copies[-1].start()
    for shift, copy in enumerate(copies):
        copy.wait()
        part = mm(out_ref[...], wbuf[shift], NN)
        if shift:
            sends[shift - 1][...] = part.astype(jnp.bfloat16)
        else:
            own_ref[...] = part


def weight_kernel(where_ref, masked_t_ref, *rest):
    pieces, (mine_ref, theirs_ref) = rest[:-2], rest[-2:]
    half, wide = mine_ref.shape[1:]
    cols = pieces[0].shape[1]
    per_piece = cols // wide
    ranks = mine_ref.shape[0] // per_piece
    core = where_ref[0] % 2
    for side, ref in ((1 - core, theirs_ref), (core, mine_ref)):
        left = masked_t_ref[pl.ds(pl.multiple_of(side * half, BLK), half), :]
        cut = pieces[-1].shape[0]
        products = [mm(left, piece[...], NN) for piece in pieces[:3]]
        products.append(
            mm(left[:, :cut], pieces[3][...], NN) + mm(left[:, cut:], pieces[4][...], NN)
        )
        for shift, part in zip(SHIFTS, products):
            first = (where_ref[1] + shift) % ranks * per_piece
            part = part.astype(jnp.bfloat16)
            for i in range(per_piece):
                ref[first + i] = part[:, i * wide : (i + 1) * wide]


def chip_sum_kernel(mine_ref, arrived_ref, out_ref):
    total = mine_ref[...].astype(jnp.float32) + arrived_ref[...].astype(jnp.float32)
    out_ref[...] = total.astype(out_ref.dtype)


def last_sum_kernel(where_ref, in_ref, keep_ref, give_ref):
    total = in_ref[0].astype(jnp.float32)
    for i in range(1, in_ref.shape[0]):
        total += in_ref[i].astype(jnp.float32)
    total = total.T
    narrow = keep_ref.shape[0]
    first = where_ref[0] % 2 == 0
    low, high = total[:narrow], total[narrow:]
    keep_ref[...] = jnp.where(first, low, high)
    give_ref[...] = jnp.where(first, high, low)


def joined_stats(parts):
    parts = parts.astype(jnp.float32)
    return parts[0:8] + parts[8:16] + parts[16:24]


def query_grad_kernel(pos_ref, pat_ref, cnt_ref, q_ref, g_ref, *rest):
    k_refs, v_refs = rest[:6], rest[6:12]
    dq_ref, kbuf, vbuf, acc, sems = rest[12:]
    pos = pos_ref[0]
    core = pos % 2
    rows, cols = q_ref.shape
    heads, blocks = cols // HD, rows // BLK
    waits = start_halo(core, k_refs, kbuf, sems, 0, True)
    waits += start_halo(core, v_refs, vbuf, sems, 5, True)
    stats = joined_stats(g_ref[rows : rows + STAT_ROWS, :])
    for copy in waits:
        copy.wait()
    for i in range(blocks):
        block = pos * blocks + i
        tok = slice(i * BLK, (i + 1) * BLK)
        turned = [
            jnp.broadcast_to(stats[x : x + 1, tok], (HD, BLK)).T for x in range(2 * heads)
        ]
        acc[...] = jnp.zeros_like(acc)

        def body(first, size):
            places = [
                pl.multiple_of((pat_ref[first + c, block] - pos * blocks + WINDOW) * BLK, BLK)
                for c in range(size)
            ]
            for h in range(heads):
                col = slice(h * HD, (h + 1) * HD)
                k = stacked(kbuf, places, col)
                s = mm(q_ref[tok, col], k, NT)
                p = jnp.exp2(s * TWO - jnp.concatenate([turned[h]] * (2 * size), 1))
                dp = mm(g_ref[tok, col], stacked(vbuf, places, col), NT)
                ds = p * (dp - jnp.concatenate([turned[heads + h]] * (2 * size), 1))
                acc[h] += mm(ds.astype(jnp.bfloat16), k, NN)

        in_chunks(cnt_ref[block], body)
        for h in range(heads):
            dq_ref[tok, h * HD : (h + 1) * HD] = (acc[h] * SCALE).astype(jnp.bfloat16)


def key_grad_kernel(pos_ref, pat_ref, cnt_ref, k_ref, v_ref, *rest):
    q_refs, g_refs = rest[:6], rest[6:12]
    dk_ref, dv_ref, qbuf, gbuf, stats, dk, dv, lists, sizes, sems = rest[12:]
    pos = pos_ref[0]
    core = pos % 2
    rows, cols = k_ref.shape
    heads, blocks = cols // HD, rows // BLK
    all_blocks = pat_ref.shape[1]
    sent_rows = rows + STAT_ROWS
    waits = start_halo(core, q_refs, qbuf, sems, 0, True)
    waits += start_halo(core, g_refs, gbuf, sems, 5, True)
    for i in range(blocks):
        sizes[i] = 0

    def from_block(near, carry):
        block = pos * blocks - WINDOW + near
        inside = (block >= 0) & (block < all_blocks)
        block = jnp.clip(block, 0, all_blocks - 1)

        def slot(j, inner):
            place = pat_ref[j, block] - pos * blocks

            @pl.when((place >= 0) & (place < blocks))
            def _():
                size = sizes[place]
                lists[place, size] = near
                sizes[place] = size + 1

            return inner

        lax.fori_loop(0, jnp.where(inside, cnt_ref[block], 0), slot, 0)
        return carry

    lax.fori_loop(0, 2 * WINDOW + blocks, from_block, 0)
    for copy in waits:
        copy.wait()
    for device in range(gbuf.shape[0] // sent_rows):
        first = device * sent_rows + rows
        both = joined_stats(gbuf[first : first + STAT_ROWS, :])
        for part in range(blocks):
            stats[device * blocks + part] = both[:, part * BLK : (part + 1) * BLK]
    for i in range(blocks):
        own = slice(i * BLK, (i + 1) * BLK)
        dk[...] = jnp.zeros_like(dk)
        dv[...] = jnp.zeros_like(dv)

        def body(first, size):
            nears = [lists[i, first + c] for c in range(size)]
            q_rows = [pl.multiple_of(near * BLK, BLK) for near in nears]
            g_rows = [
                pl.multiple_of(near // blocks * sent_rows + near % blocks * BLK, 32)
                for near in nears
            ]
            both = jnp.concatenate([stats[near] for near in nears], axis=1)
            for h in range(heads):
                col = slice(h * HD, (h + 1) * HD)
                q = stacked(qbuf, q_rows, col)
                g = stacked(gbuf, g_rows, col)
                s = mm(k_ref[own, col], q, NT)
                p = jnp.exp2(s * TWO - both[h : h + 1])
                dp = mm(v_ref[own, col], g, NT)
                ds = p * (dp - both[heads + h : heads + h + 1])
                dv[h] += mm(p.astype(jnp.bfloat16), g, NN)
                dk[h] += mm(ds.astype(jnp.bfloat16), q, NN)

        in_chunks(sizes[i], body)
        for h in range(heads):
            col = slice(h * HD, (h + 1) * HD)
            dk_ref[own, col] = (dk[h] * SCALE).astype(jnp.bfloat16)
            dv_ref[own, col] = dv[h].astype(jnp.bfloat16)


SMEM = pl.BlockSpec(memory_space=pltpu.SMEM)
VMEM = pl.BlockSpec(memory_space=pltpu.VMEM)
ANY = pl.BlockSpec(memory_space=pltpu.HBM)
PARAMS = pltpu.CompilerParams(vmem_limit_bytes=24 * 1024 * 1024)
LARGE = pltpu.CompilerParams(vmem_limit_bytes=60 * 1024 * 1024)


def shape(dims, dtype=jnp.bfloat16):
    return jax.ShapeDtypeStruct(dims, dtype)


def cost(micros):
    return pl.CostEstimate(flops=int(micros * 1.1e8), bytes_accessed=1024, transcendentals=0)


def after(value, *others):
    return lax.optimization_barrier((value,) + others)[0]


def local(
    query_heads,
    key_heads,
    value_heads,
    out_weight,
    cotangent,
    loss_mask,
    block_pattern,
    block_counts,
):
    rows, cols = query_heads.shape
    heads = cols // HD
    width = out_weight.shape[1]
    ranks = lax.axis_size("tp")
    chips = lax.axis_size("seq") // 2
    position = lax.axis_index("seq")
    where = jnp.stack([position, lax.axis_index("tp")]).astype(jnp.int32)
    tables = (where, block_pattern.T, block_counts)
    f32 = jnp.float32

    key_mate, value_mate, query_mate = (swapped(x) for x in (key_heads, value_heads, query_heads))
    key_left, key_right = shifted(key_heads, 2), shifted(key_heads, -2)
    value_after = after(value_heads, key_left, key_right)
    value_left, value_right = shifted(value_after, 2), shifted(value_after, -2)
    cot_prev, cot_next = along_tp(cotangent, 1), along_tp(cotangent, -1)
    cots = (cotangent, cot_prev, cot_next)
    cots += (along_tp(cot_next[: rows // 2], -1), along_tp(cot_prev[rows // 2 :], 1))
    keys = (key_heads, key_mate, key_left, key_right) + relayed(key_left, key_right)
    query_after = after(query_heads, value_left, value_right)
    query_left, query_right = shifted(query_after, 2), shifted(query_after, -2)
    queries = (query_heads, query_mate, query_left, query_right) + relayed(query_left, query_right)

    values = (value_heads, value_mate, value_left, value_right) + relayed(value_left, value_right)

    halo = 5 * rows
    sent_shape = shape((rows + STAT_ROWS, cols))
    head_sums = pltpu.VMEM((heads, BLK, HD), f32)
    heads_out, masked_t, sent = pl.pallas_call(
        forward_kernel,
        out_shape=(shape((rows, cols)), shape((cols, rows)), sent_shape),
        in_specs=[SMEM] * 3 + [VMEM] * 2 + [ANY] * 18,
        out_specs=(VMEM,) * 3,
        scratch_shapes=[
            pltpu.VMEM((halo, cols), jnp.bfloat16),
            pltpu.VMEM((halo, cols), jnp.bfloat16),
            pltpu.VMEM((cols, width), jnp.bfloat16),
            pltpu.VMEM((rows, width), jnp.bfloat16),
            head_sums,
            head_sums,
            head_sums,
            pltpu.VMEM((2 * heads, rows), f32),
            pltpu.SemaphoreType.DMA((16,)),
        ],
        compiler_params=LARGE,
        cost_estimate=cost(10),
        name="attention_forward",
    )(*tables, query_heads, loss_mask.reshape(1, rows), out_weight, *cots, *keys, *values)
    sent_mate = swapped(sent)
    sent_left, sent_right = shifted(sent, 2), shifted(sent, -2)

    blocks = shape((chips, cols // 2, width // chips))
    mine, theirs = pl.pallas_call(
        weight_kernel,
        out_shape=(blocks, blocks),
        in_specs=[SMEM] + [VMEM] * 6,
        out_specs=(VMEM,) * 2,
        compiler_params=PARAMS,
        cost_estimate=cost(2),
        name="weight_part",
    )(where, after(masked_t, query_left, query_right), *cots)
    arrived = swapped(theirs)

    own_out, *sends = pl.pallas_call(
        project_kernel,
        out_shape=(shape((rows, cols), f32),) + (shape((rows, cols)),) * (ranks - 1),
        in_specs=[SMEM, VMEM, ANY],
        out_specs=(VMEM,) * ranks,
        scratch_shapes=[
            pltpu.VMEM((ranks, cols, width // ranks), jnp.bfloat16),
            pltpu.SemaphoreType.DMA((ranks,)),
        ],
        compiler_params=PARAMS,
        cost_estimate=cost(2.5),
        name="project",
    )(where, after(heads_out, theirs), out_weight)

    chip_sum = pl.pallas_call(
        chip_sum_kernel,
        out_shape=blocks,
        in_specs=[VMEM, VMEM],
        out_specs=VMEM,
        compiler_params=PARAMS,
        cost_estimate=cost(1),
        name="chip_sum",
    )(mine, after(arrived, own_out))

    query_grad = pl.pallas_call(
        query_grad_kernel,
        out_shape=shape((rows, cols)),
        in_specs=[SMEM] * 3 + [VMEM] * 2 + [ANY] * 12,
        out_specs=VMEM,
        scratch_shapes=[
            pltpu.VMEM((halo, cols), jnp.bfloat16),
            pltpu.VMEM((halo, cols), jnp.bfloat16),
            head_sums,
            pltpu.SemaphoreType.DMA((10,)),
        ],
        compiler_params=LARGE,
        cost_estimate=cost(10),
        name="query_grad",
    )(*tables, after(query_heads, chip_sum), sent, *keys, *values)
    grads = (sent, sent_mate, sent_left, sent_right) + relayed(sent_left, sent_right)

    same_core = [[2 * i + c for i in range(chips)] for c in range(2)]
    spread = lax.all_to_all(
        after(chip_sum, query_grad), "seq", 0, 0, axis_index_groups=same_core, tiled=True
    )
    attended = own_out
    for step, send in enumerate(sends):
        attended = attended + along_tp(send, step + 1).astype(f32)
    attended = attended.astype(jnp.bfloat16)

    key_grad, value_grad = pl.pallas_call(
        key_grad_kernel,
        out_shape=(shape((rows, cols)), shape((rows, cols))),
        in_specs=[SMEM] * 3 + [VMEM] * 2 + [ANY] * 12,
        out_specs=(VMEM,) * 2,
        scratch_shapes=[
            pltpu.VMEM((halo, cols), jnp.bfloat16),
            pltpu.VMEM((halo + 5 * STAT_ROWS, cols), jnp.bfloat16),
            pltpu.VMEM((halo // BLK, 2 * heads, BLK), f32),
            head_sums,
            head_sums,
            pltpu.SMEM((rows // BLK, halo // BLK), jnp.int32),
            pltpu.SMEM((rows // BLK,), jnp.int32),
            pltpu.SemaphoreType.DMA((10,)),
        ],
        compiler_params=LARGE,
        cost_estimate=cost(10),
        name="key_grad",
    )(*tables, after(key_heads, attended), value_heads, *queries, *grads)

    narrow = width // chips // 2
    keep, give = pl.pallas_call(
        last_sum_kernel,
        out_shape=(shape((narrow, cols // 2), f32),) * 2,
        in_specs=[SMEM, VMEM],
        out_specs=(VMEM,) * 2,
        compiler_params=PARAMS,
        cost_estimate=cost(1),
        name="last_sum",
    )(where, after(spread, key_grad))
    got = swapped(give)

    weight_grad = jnp.where(
        position % 2 == 0,
        jnp.concatenate([keep, got], 1),
        jnp.concatenate([got, keep], 1),
    ).T
    return (attended, query_grad, key_grad, value_grad, weight_grad)


def solution(mesh):
    in_specs = (
        P("seq", "tp"),
        P("seq", "tp"),
        P("seq", "tp"),
        P("tp", None),
        P("seq", "tp"),
        P("seq"),
        P(),
        P(),
    )
    out_specs = (P("seq", "tp"), P("seq", "tp"), P("seq", "tp"), P("seq", "tp"), P("tp", "seq"))
    return jax.shard_map(local, mesh=mesh, in_specs=in_specs, out_specs=out_specs, check_vma=False)
```

```python
import math

import jax
import jax.numpy as jnp
from jax import lax
from jax.experimental import pallas as pl
from jax.experimental.pallas import tpu as pltpu
from jax.sharding import PartitionSpec as P

HD = 128
BLK = 256
WINDOW = 4
SCALE = 1.0 / math.sqrt(HD)
TWO = SCALE * math.log2(math.e)
STAT_ROWS = 32
CHUNK = 4
SHIFTS = (0, 3, 1, 2, 2)

NT = (((1,), (1,)), ((), ()))
NN = (((1,), (0,)), ((), ()))
TN = (((0,), (0,)), ((), ()))


def mm(a, b, dims):
    return lax.dot_general(a, b, dims, preferred_element_type=jnp.float32)


def shifted(value, steps):
    count = lax.axis_size("seq")
    return lax.ppermute(value, "seq", [(i, (i + steps) % count) for i in range(count)])


def swapped(value):
    return lax.ppermute(value, "seq", [(i, i ^ 1) for i in range(lax.axis_size("seq"))])


def along_tp(value, steps):
    count = lax.axis_size("tp")
    return lax.ppermute(value, "tp", [(i, (i + steps) % count) for i in range(count)])


def relayed(from_left, from_right):
    return swapped(from_left), swapped(from_right)


def start_halo(core, refs, buf, sems, first, with_own):
    own, mate, left, right, to_even, to_odd = refs
    rows = left.shape[0]

    def slot(index):
        return buf.at[pl.ds(pl.multiple_of(index * rows, 32), rows)]

    copies = [
        pltpu.make_async_copy(left, slot(0), sems.at[first]),
        pltpu.make_async_copy(right, slot(4), sems.at[first + 1]),
        pltpu.make_async_copy(mate, slot(3 - 2 * core), sems.at[first + 2]),
    ]
    if with_own:
        copies.append(pltpu.make_async_copy(own, slot(2), sems.at[first + 3]))
    for copy in copies:
        copy.start()
    even = pltpu.make_async_copy(to_even, slot(1), sems.at[first + 4])
    odd = pltpu.make_async_copy(to_odd, slot(3), sems.at[first + 4])

    @pl.when(core == 0)
    def _():
        even.start()

    @pl.when(core != 0)
    def _():
        odd.start()

    return copies + [even]


def in_chunks(count, body):
    def whole(c, carry):
        body(c * CHUNK, CHUNK)
        return carry

    lax.fori_loop(0, count // CHUNK, whole, 0)
    rest = count % CHUNK
    for size in range(1, CHUNK):

        @pl.when(rest == size)
        def _():
            body(count - size, size)


def stacked(ref, rows, col):
    return jnp.concatenate([ref[pl.ds(row, BLK), col] for row in rows], axis=0)


def folded(x, op):
    total = x[:, :HD]
    for i in range(1, x.shape[1] // HD):
        total = op(total, x[:, i * HD : (i + 1) * HD])
    return total


def forward_kernel(pos_ref, pat_ref, cnt_ref, q_ref, mask_ref, weight_hbm, *rest):
    pieces, rest = rest[:5], rest[5:]
    k_refs, v_refs = rest[:6], rest[6:12]
    outs, rest = rest[12:19], rest[19:]
    sent_ref, mine_ref, theirs_ref, own_ref, *sends = rest[:7]
    out_ref, masked_t_ref, kbuf, vbuf, wbuf, cbuf, top, total, acc, stats, sems = rest[7:]
    leaving = []

    def leave(buf):
        n = len(leaving)
        leaving.append(pltpu.make_async_copy(buf, outs[n], sems.at[16 + n]))
        leaving[-1].start()

    pos = pos_ref[0]
    core = pos % 2
    rows, cols = q_ref.shape
    heads, blocks = cols // HD, rows // BLK
    waits = start_halo(core, k_refs, kbuf, sems, 0, True)
    waits += start_halo(core, v_refs, vbuf, sems, 5, True)
    ranks = wbuf.shape[1] // cols
    later = [pltpu.make_async_copy(weight_hbm, wbuf, sems.at[10])]
    for x, (piece, shift) in enumerate(zip(pieces, SHIFTS)):
        low = 0 if x < ranks else rows - piece.shape[0]
        place = cbuf.at[
            pl.ds(low, piece.shape[0]),
            pl.ds(pl.multiple_of((pos_ref[1] + shift) % ranks * cols, HD), cols),
        ]
        later.append(pltpu.make_async_copy(piece, place, sems.at[11 + x]))
    for copy in later:
        copy.start()
    for copy in waits:
        copy.wait()
    for i in range(blocks):
        block = pos * blocks + i
        tok = slice(i * BLK, (i + 1) * BLK)
        top[...] = jnp.full_like(top, -1e30)
        total[...] = jnp.zeros_like(total)
        acc[...] = jnp.zeros_like(acc)

        def body(first, size):
            places = [
                pl.multiple_of((pat_ref[first + c, block] - pos * blocks + WINDOW) * BLK, BLK)
                for c in range(size)
            ]
            for h in range(heads):
                col = slice(h * HD, (h + 1) * HD)
                s = mm(q_ref[tok, col], stacked(kbuf, places, col), NT)
                high = jnp.max(folded(s, jnp.maximum), axis=1, keepdims=True) * TWO
                old = top[h]
                new = jnp.maximum(old, high)
                p = jnp.exp2(s * TWO - jnp.concatenate([new] * (2 * size), 1))
                fade = jnp.exp2(old - new)
                top[h] = new
                total[h] = total[h] * fade + folded(p, jnp.add)
                acc[h] = acc[h] * fade + mm(
                    p.astype(jnp.bfloat16), stacked(vbuf, places, col), NN
                )

        in_chunks(cnt_ref[block], body)
        for h in range(heads):
            col = slice(h * HD, (h + 1) * HD)
            whole = jnp.sum(total[h], axis=1, keepdims=True)
            out = acc[h] * (1.0 / whole)
            rounded = out.astype(jnp.bfloat16)
            out_ref[tok, col] = rounded
            masked_t_ref[col, tok] = jnp.where(mask_ref[:, tok] == 1, out.T, 0.0).astype(
                jnp.bfloat16
            )
            lse = top[h] + jnp.log(whole) * math.log2(math.e)
            stats[h : h + 1, tok] = lse.T[0:1]
    for copy in later:
        copy.wait()
    kept = jnp.broadcast_to(mask_ref[...], (HD, rows)).astype(jnp.float32).T == 1.0
    half = cols // 2
    for part in range(2):
        grad = mm(cbuf[...], wbuf[part * half : (part + 1) * half, :], NT)
        for h in range(half // HD):
            head = part * (half // HD) + h
            col = slice(head * HD, (head + 1) * HD)
            one = jnp.where(kept, grad[:, h * HD : (h + 1) * HD], 0.0).astype(jnp.bfloat16)
            sent_ref[0:rows, col] = one
            dots = one.astype(jnp.float32) * out_ref[:, col].astype(jnp.float32)
            stats[heads + head : heads + head + 1, :] = jnp.sum(dots.T, axis=0, keepdims=True)
    whole = stats[...]
    high = whole.astype(jnp.bfloat16).astype(jnp.float32)
    middle = (whole - high).astype(jnp.bfloat16).astype(jnp.float32)
    low = whole - high - middle
    parts = jnp.concatenate([high, middle, low, jnp.zeros_like(low)], axis=0)
    sent_ref[rows : rows + STAT_ROWS, :] = parts.astype(jnp.bfloat16)
    leave(sent_ref)
    side, wide = mine_ref.shape[1:]
    for which, ref in ((core, mine_ref), (1 - core, theirs_ref)):
        left = masked_t_ref[pl.ds(pl.multiple_of(which * side, side), side), :]
        for j in range(ranks):
            part = mm(left, cbuf[:, j * cols : (j + 1) * cols], NN).astype(jnp.bfloat16)
            for x in range(cols // wide):
                ref[j * (cols // wide) + x] = part[:, x * wide : (x + 1) * wide]
        leave(ref)
    for shift in range(ranks):
        first = pl.multiple_of((pos_ref[1] + shift) % ranks * cols, HD)
        part = mm(out_ref[...], wbuf[:, pl.ds(first, cols)], NN)
        ref = sends[shift - 1] if shift else own_ref
        ref[...] = part.astype(ref.dtype)
        leave(ref)
    for copy in leaving:
        copy.wait()


def chip_sum_kernel(mine_ref, arrived_ref, out_ref):
    total = mine_ref[...].astype(jnp.float32) + arrived_ref[...].astype(jnp.float32)
    out_ref[...] = total.astype(out_ref.dtype)


def last_sum_kernel(where_ref, in_ref, keep_ref, give_ref):
    total = in_ref[0].astype(jnp.float32)
    for i in range(1, in_ref.shape[0]):
        total += in_ref[i].astype(jnp.float32)
    total = total.T
    narrow = keep_ref.shape[0]
    first = where_ref[0] % 2 == 0
    low, high = total[:narrow], total[narrow:]
    keep_ref[...] = jnp.where(first, low, high)
    give_ref[...] = jnp.where(first, high, low)


def joined_stats(parts):
    parts = parts.astype(jnp.float32)
    return parts[0:8] + parts[8:16] + parts[16:24]


def query_grad_kernel(pos_ref, pat_ref, cnt_ref, q_ref, g_ref, *rest):
    k_refs, v_refs = rest[:6], rest[6:12]
    dq_ref, kbuf, vbuf, acc, sems = rest[12:]
    pos = pos_ref[0]
    core = pos % 2
    rows, cols = q_ref.shape
    heads, blocks = cols // HD, rows // BLK
    waits = start_halo(core, k_refs, kbuf, sems, 0, True)
    waits += start_halo(core, v_refs, vbuf, sems, 5, True)
    stats = joined_stats(g_ref[rows : rows + STAT_ROWS, :])
    for copy in waits:
        copy.wait()
    for i in range(blocks):
        block = pos * blocks + i
        tok = slice(i * BLK, (i + 1) * BLK)
        turned = [
            jnp.broadcast_to(stats[x : x + 1, tok], (HD, BLK)).T for x in range(2 * heads)
        ]
        acc[...] = jnp.zeros_like(acc)

        def body(first, size):
            places = [
                pl.multiple_of((pat_ref[first + c, block] - pos * blocks + WINDOW) * BLK, BLK)
                for c in range(size)
            ]
            for h in range(heads):
                col = slice(h * HD, (h + 1) * HD)
                k = stacked(kbuf, places, col)
                s = mm(q_ref[tok, col], k, NT)
                p = jnp.exp2(s * TWO - jnp.concatenate([turned[h]] * (2 * size), 1))
                dp = mm(g_ref[tok, col], stacked(vbuf, places, col), NT)
                ds = p * (dp - jnp.concatenate([turned[heads + h]] * (2 * size), 1))
                acc[h] += mm(ds.astype(jnp.bfloat16), k, NN)

        in_chunks(cnt_ref[block], body)
        for h in range(heads):
            dq_ref[tok, h * HD : (h + 1) * HD] = (acc[h] * SCALE).astype(jnp.bfloat16)


def key_grad_kernel(pos_ref, pat_ref, cnt_ref, k_ref, v_ref, *rest):
    q_refs, g_refs = rest[:6], rest[6:12]
    dk_ref, dv_ref, qbuf, gbuf, stats, dk, dv, lists, sizes, sems = rest[12:]
    pos = pos_ref[0]
    core = pos % 2
    rows, cols = k_ref.shape
    heads, blocks = cols // HD, rows // BLK
    all_blocks = pat_ref.shape[1]
    sent_rows = rows + STAT_ROWS
    waits = start_halo(core, q_refs, qbuf, sems, 0, True)
    waits += start_halo(core, g_refs, gbuf, sems, 5, True)
    for i in range(blocks):
        sizes[i] = 0

    def from_block(near, carry):
        block = pos * blocks - WINDOW + near
        inside = (block >= 0) & (block < all_blocks)
        block = jnp.clip(block, 0, all_blocks - 1)

        def slot(j, inner):
            place = pat_ref[j, block] - pos * blocks

            @pl.when((place >= 0) & (place < blocks))
            def _():
                size = sizes[place]
                lists[place, size] = near
                sizes[place] = size + 1

            return inner

        lax.fori_loop(0, jnp.where(inside, cnt_ref[block], 0), slot, 0)
        return carry

    lax.fori_loop(0, 2 * WINDOW + blocks, from_block, 0)
    for copy in waits:
        copy.wait()
    for device in range(gbuf.shape[0] // sent_rows):
        first = device * sent_rows + rows
        both = joined_stats(gbuf[first : first + STAT_ROWS, :])
        for part in range(blocks):
            stats[device * blocks + part] = both[:, part * BLK : (part + 1) * BLK]
    for i in range(blocks):
        own = slice(i * BLK, (i + 1) * BLK)
        dk[...] = jnp.zeros_like(dk)
        dv[...] = jnp.zeros_like(dv)

        def body(first, size):
            nears = [lists[i, first + c] for c in range(size)]
            q_rows = [pl.multiple_of(near * BLK, BLK) for near in nears]
            g_rows = [
                pl.multiple_of(near // blocks * sent_rows + near % blocks * BLK, 32)
                for near in nears
            ]
            both = jnp.concatenate([stats[near] for near in nears], axis=1)
            for h in range(heads):
                col = slice(h * HD, (h + 1) * HD)
                q = stacked(qbuf, q_rows, col)
                g = stacked(gbuf, g_rows, col)
                s = mm(k_ref[own, col], q, NT)
                p = jnp.exp2(s * TWO - both[h : h + 1])
                dp = mm(v_ref[own, col], g, NT)
                ds = p * (dp - both[heads + h : heads + h + 1])
                dv[h] += mm(p.astype(jnp.bfloat16), g, NN)
                dk[h] += mm(ds.astype(jnp.bfloat16), q, NN)

        in_chunks(sizes[i], body)
        for h in range(heads):
            col = slice(h * HD, (h + 1) * HD)
            dk_ref[own, col] = (dk[h] * SCALE).astype(jnp.bfloat16)
            dv_ref[own, col] = dv[h].astype(jnp.bfloat16)


SMEM = pl.BlockSpec(memory_space=pltpu.SMEM)
VMEM = pl.BlockSpec(memory_space=pltpu.VMEM)
ANY = pl.BlockSpec(memory_space=pltpu.HBM)
PARAMS = pltpu.CompilerParams(vmem_limit_bytes=24 * 1024 * 1024)
LARGE = pltpu.CompilerParams(vmem_limit_bytes=60 * 1024 * 1024)


def shape(dims, dtype=jnp.bfloat16):
    return jax.ShapeDtypeStruct(dims, dtype)


def cost(micros):
    return pl.CostEstimate(flops=int(micros * 1.1e8), bytes_accessed=1024, transcendentals=0)


def after(value, *others):
    return lax.optimization_barrier((value,) + others)[0]


def local(
    query_heads,
    key_heads,
    value_heads,
    out_weight,
    cotangent,
    loss_mask,
    block_pattern,
    block_counts,
):
    rows, cols = query_heads.shape
    heads = cols // HD
    width = out_weight.shape[1]
    ranks = lax.axis_size("tp")
    chips = lax.axis_size("seq") // 2
    position = lax.axis_index("seq")
    where = jnp.stack([position, lax.axis_index("tp")]).astype(jnp.int32)
    tables = (where, block_pattern.T, block_counts)
    f32 = jnp.float32

    key_mate, value_mate, query_mate = (swapped(x) for x in (key_heads, value_heads, query_heads))
    key_left, key_right = shifted(key_heads, 2), shifted(key_heads, -2)
    value_after = after(value_heads, key_left, key_right)
    value_left, value_right = shifted(value_after, 2), shifted(value_after, -2)
    cot_prev, cot_next = along_tp(cotangent, 1), along_tp(cotangent, -1)
    cots = (cotangent, cot_prev, cot_next)
    cots += (along_tp(cot_next[: rows // 2], -1), along_tp(cot_prev[rows // 2 :], 1))
    keys = (key_heads, key_mate, key_left, key_right) + relayed(key_left, key_right)
    query_after = after(query_heads, value_left, value_right)
    query_left, query_right = shifted(query_after, 2), shifted(query_after, -2)
    queries = (query_heads, query_mate, query_left, query_right) + relayed(query_left, query_right)

    values = (value_heads, value_mate, value_left, value_right) + relayed(value_left, value_right)

    halo = 5 * rows
    sent_shape = shape((rows + STAT_ROWS, cols))
    head_sums = pltpu.VMEM((heads, BLK, HD), f32)
    blocks = shape((chips, cols // 2, width // chips))
    made = (sent_shape, blocks, blocks, shape((rows, cols), f32)) + (shape((rows, cols)),) * 3
    sent, mine, theirs, own_out, *sends = pl.pallas_call(
        forward_kernel,
        out_shape=made,
        in_specs=[SMEM] * 3 + [VMEM] * 2 + [ANY] * 18,
        out_specs=(ANY,) * 7,
        scratch_shapes=[pltpu.VMEM(x.shape, x.dtype) for x in made]
        + [
            pltpu.VMEM((rows, cols), jnp.bfloat16),
            pltpu.VMEM((cols, rows), jnp.bfloat16),
            pltpu.VMEM((halo, cols), jnp.bfloat16),
            pltpu.VMEM((halo, cols), jnp.bfloat16),
            pltpu.VMEM((cols, width), jnp.bfloat16),
            pltpu.VMEM((rows, width), jnp.bfloat16),
            head_sums,
            head_sums,
            head_sums,
            pltpu.VMEM((2 * heads, rows), f32),
            pltpu.SemaphoreType.DMA((23,)),
        ],
        compiler_params=LARGE,
        cost_estimate=cost(10),
        name="attention_forward",
    )(*tables, query_heads, loss_mask.reshape(1, rows), out_weight, *cots, *keys, *values)
    sent_mate = swapped(sent)
    sent_left, sent_right = shifted(sent, 2), shifted(sent, -2)
    arrived = swapped(after(theirs, query_left, query_right))
    parts = [along_tp(send, step + 1) for step, send in enumerate(sends)]

    chip_sum = pl.pallas_call(
        chip_sum_kernel,
        out_shape=blocks,
        in_specs=[VMEM, VMEM],
        out_specs=VMEM,
        compiler_params=PARAMS,
        cost_estimate=cost(1),
        name="chip_sum",
    )(mine, arrived)

    query_grad = pl.pallas_call(
        query_grad_kernel,
        out_shape=shape((rows, cols)),
        in_specs=[SMEM] * 3 + [VMEM] * 2 + [ANY] * 12,
        out_specs=VMEM,
        scratch_shapes=[
            pltpu.VMEM((halo, cols), jnp.bfloat16),
            pltpu.VMEM((halo, cols), jnp.bfloat16),
            head_sums,
            pltpu.SemaphoreType.DMA((10,)),
        ],
        compiler_params=LARGE,
        cost_estimate=cost(10),
        name="query_grad",
    )(*tables, after(query_heads, chip_sum), sent, *keys, *values)
    grads = (sent, sent_mate, sent_left, sent_right) + relayed(sent_left, sent_right)

    same_core = [[2 * i + c for i in range(chips)] for c in range(2)]
    spread = lax.all_to_all(
        after(chip_sum, query_grad), "seq", 0, 0, axis_index_groups=same_core, tiled=True
    )
    key_grad, value_grad = pl.pallas_call(
        key_grad_kernel,
        out_shape=(shape((rows, cols)), shape((rows, cols))),
        in_specs=[SMEM] * 3 + [VMEM] * 2 + [ANY] * 12,
        out_specs=(VMEM,) * 2,
        scratch_shapes=[
            pltpu.VMEM((halo, cols), jnp.bfloat16),
            pltpu.VMEM((halo + 5 * STAT_ROWS, cols), jnp.bfloat16),
            pltpu.VMEM((halo // BLK, 2 * heads, BLK), f32),
            head_sums,
            head_sums,
            pltpu.SMEM((rows // BLK, halo // BLK), jnp.int32),
            pltpu.SMEM((rows // BLK,), jnp.int32),
            pltpu.SemaphoreType.DMA((10,)),
        ],
        compiler_params=LARGE,
        cost_estimate=cost(10),
        name="key_grad",
    )(*tables, after(key_heads, *parts), value_heads, *queries, *grads)

    narrow = width // chips // 2
    keep, give = pl.pallas_call(
        last_sum_kernel,
        out_shape=(shape((narrow, cols // 2), f32),) * 2,
        in_specs=[SMEM, VMEM],
        out_specs=(VMEM,) * 2,
        compiler_params=PARAMS,
        cost_estimate=cost(1),
        name="last_sum",
    )(where, after(spread, key_grad))
    got = swapped(give)

    attended = after(own_out, key_grad)
    for part in parts:
        attended = attended + part.astype(f32)
    attended = attended.astype(jnp.bfloat16)
    weight_grad = jnp.where(
        position % 2 == 0,
        jnp.concatenate([keep, got], 1),
        jnp.concatenate([got, keep], 1),
    ).T
    return (attended, query_grad, key_grad, value_grad, weight_grad)


def solution(mesh):
    in_specs = (
        P("seq", "tp"),
        P("seq", "tp"),
        P("seq", "tp"),
        P("tp", None),
        P("seq", "tp"),
        P("seq"),
        P(),
        P(),
    )
    out_specs = (P("seq", "tp"), P("seq", "tp"), P("seq", "tp"), P("seq", "tp"), P("tp", "seq"))
    return jax.shard_map(local, mesh=mesh, in_specs=in_specs, out_specs=out_specs, check_vma=False)
```

```python
import math

import jax
import jax.numpy as jnp
from jax import lax
from jax.experimental import pallas as pl
from jax.experimental.pallas import tpu as pltpu
from jax.sharding import PartitionSpec as P

HD = 128
BLK = 256
WINDOW = 4
SCALE = 1.0 / math.sqrt(HD)
TWO = SCALE * math.log2(math.e)
STAT_ROWS = 32
CHUNK = 4
SHIFTS = (0, 3, 1, 2, 2)

NT = (((1,), (1,)), ((), ()))
NN = (((1,), (0,)), ((), ()))
TN = (((0,), (0,)), ((), ()))


def mm(a, b, dims):
    return lax.dot_general(a, b, dims, preferred_element_type=jnp.float32)


def shifted(value, steps):
    count = lax.axis_size("seq")
    return lax.ppermute(value, "seq", [(i, (i + steps) % count) for i in range(count)])


def swapped(value):
    return lax.ppermute(value, "seq", [(i, i ^ 1) for i in range(lax.axis_size("seq"))])


def along_tp(value, steps):
    count = lax.axis_size("tp")
    return lax.ppermute(value, "tp", [(i, (i + steps) % count) for i in range(count)])


def relayed(from_left, from_right):
    return swapped(from_left), swapped(from_right)


def start_halo(core, refs, buf, sems, first, with_own):
    own, mate, left, right, to_even, to_odd = refs
    rows = left.shape[0]

    def slot(index):
        return buf.at[pl.ds(pl.multiple_of(index * rows, 32), rows)]

    copies = [
        pltpu.make_async_copy(left, slot(0), sems.at[first]),
        pltpu.make_async_copy(right, slot(4), sems.at[first + 1]),
        pltpu.make_async_copy(mate, slot(3 - 2 * core), sems.at[first + 2]),
    ]
    if with_own:
        copies.append(pltpu.make_async_copy(own, slot(2), sems.at[first + 3]))
    for copy in copies:
        copy.start()
    even = pltpu.make_async_copy(to_even, slot(1), sems.at[first + 4])
    odd = pltpu.make_async_copy(to_odd, slot(3), sems.at[first + 4])

    @pl.when(core == 0)
    def _():
        even.start()

    @pl.when(core != 0)
    def _():
        odd.start()

    return copies + [even]


def in_chunks(count, body):
    def whole(c, carry):
        body(c * CHUNK, CHUNK)
        return carry

    lax.fori_loop(0, count // CHUNK, whole, 0)
    rest = count % CHUNK
    for size in range(1, CHUNK):

        @pl.when(rest == size)
        def _():
            body(count - size, size)


def stacked(ref, rows, col):
    return jnp.concatenate([ref[pl.ds(row, BLK), col] for row in rows], axis=0)


def folded(x, op):
    total = x[:, :HD]
    for i in range(1, x.shape[1] // HD):
        total = op(total, x[:, i * HD : (i + 1) * HD])
    return total


def forward_kernel(pos_ref, pat_ref, cnt_ref, q_ref, mask_ref, weight_hbm, *rest):
    pieces, rest = rest[:5], rest[5:]
    k_refs, v_refs = rest[:6], rest[6:12]
    outs, rest = rest[12:19], rest[19:]
    sent_ref, mine_ref, theirs_ref, own_ref, *sends = rest[:7]
    out_ref, masked_ref, kbuf, vbuf, wbuf, cbuf, top, total, acc, stats, sems = rest[7:]
    leaving = []

    def leave(buf):
        n = len(leaving)
        leaving.append(pltpu.make_async_copy(buf, outs[n], sems.at[16 + n]))
        leaving[-1].start()

    pos = pos_ref[0]
    core = pos % 2
    rows, cols = q_ref.shape
    heads, blocks = cols // HD, rows // BLK
    waits = start_halo(core, k_refs, kbuf, sems, 0, True)
    waits += start_halo(core, v_refs, vbuf, sems, 5, True)
    ranks = wbuf.shape[1] // cols
    later = [pltpu.make_async_copy(weight_hbm, wbuf, sems.at[10])]
    for x, (piece, shift) in enumerate(zip(pieces, SHIFTS)):
        low = 0 if x < ranks else rows - piece.shape[0]
        place = cbuf.at[
            pl.ds(low, piece.shape[0]),
            pl.ds(pl.multiple_of((pos_ref[1] + shift) % ranks * cols, HD), cols),
        ]
        later.append(pltpu.make_async_copy(piece, place, sems.at[11 + x]))
    for copy in waits:
        copy.wait()
    for copy in later:
        copy.start()
    for i in range(blocks):
        block = pos * blocks + i
        tok = slice(i * BLK, (i + 1) * BLK)
        top[...] = jnp.full_like(top, -1e30)
        total[...] = jnp.zeros_like(total)
        acc[...] = jnp.zeros_like(acc)

        def body(first, size):
            places = [
                pl.multiple_of((pat_ref[first + c, block] - pos * blocks + WINDOW) * BLK, BLK)
                for c in range(size)
            ]
            for h in range(heads):
                col = slice(h * HD, (h + 1) * HD)
                s = mm(q_ref[tok, col], stacked(kbuf, places, col), NT)
                high = jnp.max(folded(s, jnp.maximum), axis=1, keepdims=True) * TWO
                old = top[h]
                new = jnp.maximum(old, high)
                p = jnp.exp2(s * TWO - jnp.concatenate([new] * (2 * size), 1))
                fade = jnp.exp2(old - new)
                top[h] = new
                total[h] = total[h] * fade + folded(p, jnp.add)
                acc[h] = acc[h] * fade + mm(
                    p.astype(jnp.bfloat16), stacked(vbuf, places, col), NN
                )

        in_chunks(cnt_ref[block], body)
        for h in range(heads):
            col = slice(h * HD, (h + 1) * HD)
            whole = jnp.sum(total[h], axis=1, keepdims=True)
            out = acc[h] * (1.0 / whole)
            rounded = out.astype(jnp.bfloat16)
            out_ref[tok, col] = rounded
            lse = top[h] + jnp.log(whole) * math.log2(math.e)
            stats[h : h + 1, tok] = lse.T[0:1]
    for copy in later:
        copy.wait()
    kept = jnp.broadcast_to(mask_ref[...], (HD, rows)).astype(jnp.float32).T == 1.0
    half = cols // 2
    for part in range(2):
        grad = mm(cbuf[...], wbuf[part * half : (part + 1) * half, :], NT)
        for h in range(half // HD):
            head = part * (half // HD) + h
            col = slice(head * HD, (head + 1) * HD)
            one = jnp.where(kept, grad[:, h * HD : (h + 1) * HD], 0.0).astype(jnp.bfloat16)
            sent_ref[0:rows, col] = one
            masked_ref[:, col] = jnp.where(kept, out_ref[:, col].astype(jnp.float32), 0.0).astype(
                jnp.bfloat16
            )
            dots = one.astype(jnp.float32) * out_ref[:, col].astype(jnp.float32)
            stats[heads + head : heads + head + 1, :] = jnp.sum(dots.T, axis=0, keepdims=True)
    whole = stats[...]
    high = whole.astype(jnp.bfloat16).astype(jnp.float32)
    middle = (whole - high).astype(jnp.bfloat16).astype(jnp.float32)
    low = whole - high - middle
    parts = jnp.concatenate([high, middle, low, jnp.zeros_like(low)], axis=0)
    sent_ref[rows : rows + STAT_ROWS, :] = parts.astype(jnp.bfloat16)
    leave(sent_ref)
    narrow = mine_ref.shape[1]
    count = mine_ref.shape[0] // ranks
    for j in range(ranks):
        part = mm(cbuf[:, j * cols : (j + 1) * cols], masked_ref[...], TN).astype(jnp.bfloat16)
        for x in range(count):
            low = part[2 * x * narrow : (2 * x + 1) * narrow]
            high = part[(2 * x + 1) * narrow : (2 * x + 2) * narrow]
            mine_ref[j * count + x] = jnp.where(core == 0, low, high)
            theirs_ref[j * count + x] = jnp.where(core == 0, high, low)
    leave(mine_ref)
    leave(theirs_ref)
    for shift in range(ranks):
        first = pl.multiple_of((pos_ref[1] + shift) % ranks * cols, HD)
        part = mm(out_ref[...], wbuf[:, pl.ds(first, cols)], NN)
        ref = sends[shift - 1] if shift else own_ref
        ref[...] = part.astype(ref.dtype)
        leave(ref)
    for copy in leaving:
        copy.wait()


def chip_sum_kernel(mine_ref, arrived_ref, out_ref):
    total = mine_ref[...].astype(jnp.float32) + arrived_ref[...].astype(jnp.float32)
    out_ref[...] = total.astype(out_ref.dtype)


def last_sum_kernel(in_ref, out_ref):
    total = in_ref[0].astype(jnp.float32)
    for i in range(1, in_ref.shape[0]):
        total += in_ref[i].astype(jnp.float32)
    out_ref[...] = total


def joined_stats(parts):
    parts = parts.astype(jnp.float32)
    return parts[0:8] + parts[8:16] + parts[16:24]


def query_grad_kernel(pos_ref, pat_ref, cnt_ref, q_ref, g_ref, *rest):
    k_refs, v_refs = rest[:6], rest[6:12]
    dq_ref, kbuf, vbuf, acc, sems = rest[12:]
    pos = pos_ref[0]
    core = pos % 2
    rows, cols = q_ref.shape
    heads, blocks = cols // HD, rows // BLK
    waits = start_halo(core, k_refs, kbuf, sems, 0, True)
    waits += start_halo(core, v_refs, vbuf, sems, 5, True)
    stats = joined_stats(g_ref[rows : rows + STAT_ROWS, :])
    for copy in waits:
        copy.wait()
    for i in range(blocks):
        block = pos * blocks + i
        tok = slice(i * BLK, (i + 1) * BLK)
        turned = [
            jnp.broadcast_to(stats[x : x + 1, tok], (HD, BLK)).T for x in range(2 * heads)
        ]
        acc[...] = jnp.zeros_like(acc)

        def body(first, size):
            places = [
                pl.multiple_of((pat_ref[first + c, block] - pos * blocks + WINDOW) * BLK, BLK)
                for c in range(size)
            ]
            for h in range(heads):
                col = slice(h * HD, (h + 1) * HD)
                k = stacked(kbuf, places, col)
                s = mm(q_ref[tok, col], k, NT)
                p = jnp.exp2(s * TWO - jnp.concatenate([turned[h]] * (2 * size), 1))
                dp = mm(g_ref[tok, col], stacked(vbuf, places, col), NT)
                ds = p * (dp - jnp.concatenate([turned[heads + h]] * (2 * size), 1))
                acc[h] += mm(ds.astype(jnp.bfloat16), k, NN)

        in_chunks(cnt_ref[block], body)
        for h in range(heads):
            dq_ref[tok, h * HD : (h + 1) * HD] = (acc[h] * SCALE).astype(jnp.bfloat16)


def key_grad_kernel(pos_ref, pat_ref, cnt_ref, k_ref, v_ref, *rest):
    q_refs, g_refs, parts, rest = rest[:6], rest[6:12], rest[12:16], rest[16:]
    dk_ref, dv_ref, attended_ref, qbuf, gbuf, stats, dk, dv = rest[:8]
    lists, sizes, own_part, more, sems = rest[8:]
    pos = pos_ref[0]
    core = pos % 2
    rows, cols = k_ref.shape
    heads, blocks = cols // HD, rows // BLK
    all_blocks = pat_ref.shape[1]
    sent_rows = rows + STAT_ROWS
    waits = start_halo(core, q_refs, qbuf, sems, 0, True)
    waits += start_halo(core, g_refs, gbuf, sems, 5, True)
    for i in range(blocks):
        sizes[i] = 0

    def from_block(near, carry):
        block = pos * blocks - WINDOW + near
        inside = (block >= 0) & (block < all_blocks)
        block = jnp.clip(block, 0, all_blocks - 1)

        def slot(j, inner):
            place = pat_ref[j, block] - pos * blocks

            @pl.when((place >= 0) & (place < blocks))
            def _():
                size = sizes[place]
                lists[place, size] = near
                sizes[place] = size + 1

            return inner

        lax.fori_loop(0, jnp.where(inside, cnt_ref[block], 0), slot, 0)
        return carry

    lax.fori_loop(0, 2 * WINDOW + blocks, from_block, 0)
    for copy in waits:
        copy.wait()
    later = [pltpu.make_async_copy(parts[0], own_part, sems.at[10])]
    for x, part in enumerate(parts[1:]):
        later.append(pltpu.make_async_copy(part, more.at[x], sems.at[11 + x]))
    for copy in later:
        copy.start()
    for device in range(gbuf.shape[0] // sent_rows):
        first = device * sent_rows + rows
        both = joined_stats(gbuf[first : first + STAT_ROWS, :])
        for part in range(blocks):
            stats[device * blocks + part] = both[:, part * BLK : (part + 1) * BLK]
    for i in range(blocks):
        own = slice(i * BLK, (i + 1) * BLK)
        dk[...] = jnp.zeros_like(dk)
        dv[...] = jnp.zeros_like(dv)

        def body(first, size):
            nears = [lists[i, first + c] for c in range(size)]
            q_rows = [pl.multiple_of(near * BLK, BLK) for near in nears]
            g_rows = [
                pl.multiple_of(near // blocks * sent_rows + near % blocks * BLK, 32)
                for near in nears
            ]
            both = jnp.concatenate([stats[near] for near in nears], axis=1)
            for h in range(heads):
                col = slice(h * HD, (h + 1) * HD)
                q = stacked(qbuf, q_rows, col)
                g = stacked(gbuf, g_rows, col)
                s = mm(k_ref[own, col], q, NT)
                p = jnp.exp2(s * TWO - both[h : h + 1])
                dp = mm(v_ref[own, col], g, NT)
                ds = p * (dp - both[heads + h : heads + h + 1])
                dv[h] += mm(p.astype(jnp.bfloat16), g, NN)
                dk[h] += mm(ds.astype(jnp.bfloat16), q, NN)

        in_chunks(sizes[i], body)
        for h in range(heads):
            col = slice(h * HD, (h + 1) * HD)
            dk_ref[own, col] = (dk[h] * SCALE).astype(jnp.bfloat16)
            dv_ref[own, col] = dv[h].astype(jnp.bfloat16)
    for copy in later:
        copy.wait()
    whole = own_part[...]
    for x in range(more.shape[0]):
        whole += more[x].astype(jnp.float32)
    attended_ref[...] = whole.astype(jnp.bfloat16)


SMEM = pl.BlockSpec(memory_space=pltpu.SMEM)
VMEM = pl.BlockSpec(memory_space=pltpu.VMEM)
ANY = pl.BlockSpec(memory_space=pltpu.HBM)
PARAMS = pltpu.CompilerParams(vmem_limit_bytes=24 * 1024 * 1024)
LARGE = pltpu.CompilerParams(vmem_limit_bytes=60 * 1024 * 1024)


def shape(dims, dtype=jnp.bfloat16):
    return jax.ShapeDtypeStruct(dims, dtype)


def cost(micros):
    return pl.CostEstimate(flops=int(micros * 1.1e8), bytes_accessed=1024, transcendentals=0)


def after(value, *others):
    return lax.optimization_barrier((value,) + others)[0]


def local(
    query_heads,
    key_heads,
    value_heads,
    out_weight,
    cotangent,
    loss_mask,
    block_pattern,
    block_counts,
):
    rows, cols = query_heads.shape
    heads = cols // HD
    width = out_weight.shape[1]
    ranks = lax.axis_size("tp")
    chips = lax.axis_size("seq") // 2
    position = lax.axis_index("seq")
    where = jnp.stack([position, lax.axis_index("tp")]).astype(jnp.int32)
    tables = (where, block_pattern.T, block_counts)
    f32 = jnp.float32

    key_mate, value_mate, query_mate = (swapped(x) for x in (key_heads, value_heads, query_heads))
    key_left, key_right = shifted(key_heads, 2), shifted(key_heads, -2)
    value_after = after(value_heads, key_left, key_right)
    value_left, value_right = shifted(value_after, 2), shifted(value_after, -2)
    cot_prev, cot_next = along_tp(cotangent, 1), along_tp(cotangent, -1)
    cots = (cotangent, cot_prev, cot_next)
    cots += (along_tp(cot_next[: rows // 2], -1), along_tp(cot_prev[rows // 2 :], 1))
    keys = (key_heads, key_mate, key_left, key_right) + relayed(key_left, key_right)
    query_after = after(query_heads, value_left, value_right)
    query_left, query_right = shifted(query_after, 2), shifted(query_after, -2)
    queries = (query_heads, query_mate, query_left, query_right) + relayed(query_left, query_right)

    values = (value_heads, value_mate, value_left, value_right) + relayed(value_left, value_right)

    halo = 5 * rows
    sent_shape = shape((rows + STAT_ROWS, cols))
    head_sums = pltpu.VMEM((heads, BLK, HD), f32)
    blocks = shape((chips, width // chips // 2, cols))
    made = (sent_shape, blocks, blocks, shape((rows, cols), f32)) + (shape((rows, cols)),) * 3
    sent, mine, theirs, own_out, *sends = pl.pallas_call(
        forward_kernel,
        out_shape=made,
        in_specs=[SMEM] * 3 + [VMEM] * 2 + [ANY] * 18,
        out_specs=(ANY,) * 7,
        scratch_shapes=[pltpu.VMEM(x.shape, x.dtype) for x in made]
        + [
            pltpu.VMEM((rows, cols), jnp.bfloat16),
            pltpu.VMEM((rows, cols), jnp.bfloat16),
            pltpu.VMEM((halo, cols), jnp.bfloat16),
            pltpu.VMEM((halo, cols), jnp.bfloat16),
            pltpu.VMEM((cols, width), jnp.bfloat16),
            pltpu.VMEM((rows, width), jnp.bfloat16),
            head_sums,
            head_sums,
            head_sums,
            pltpu.VMEM((2 * heads, rows), f32),
            pltpu.SemaphoreType.DMA((23,)),
        ],
        compiler_params=LARGE,
        cost_estimate=cost(10),
        name="attention_forward",
    )(*tables, query_heads, loss_mask.reshape(1, rows), out_weight, *cots, *keys, *values)
    sent_mate = swapped(sent)
    sent_left, sent_right = shifted(sent, 2), shifted(sent, -2)
    arrived = swapped(after(theirs, query_left, query_right))
    parts = [along_tp(send, step + 1) for step, send in enumerate(sends)]

    some = pl.BlockSpec((chips // 4,) + blocks.shape[1:], lambda i: (i, 0, 0))
    chip_sum = pl.pallas_call(
        chip_sum_kernel,
        grid=(4,),
        out_shape=blocks,
        in_specs=[some, some],
        out_specs=some,
        compiler_params=PARAMS,
        cost_estimate=cost(1),
        name="chip_sum",
    )(mine, arrived)

    query_grad = pl.pallas_call(
        query_grad_kernel,
        out_shape=shape((rows, cols)),
        in_specs=[SMEM] * 3 + [VMEM] * 2 + [ANY] * 12,
        out_specs=VMEM,
        scratch_shapes=[
            pltpu.VMEM((halo, cols), jnp.bfloat16),
            pltpu.VMEM((halo, cols), jnp.bfloat16),
            head_sums,
            pltpu.SemaphoreType.DMA((10,)),
        ],
        compiler_params=LARGE,
        cost_estimate=cost(10),
        name="query_grad",
    )(*tables, after(query_heads, chip_sum), sent, *keys, *values)
    grads = (sent, sent_mate, sent_left, sent_right) + relayed(sent_left, sent_right)

    same_core = [[2 * i + c for i in range(chips)] for c in range(2)]
    spread = lax.all_to_all(
        after(chip_sum, query_grad), "seq", 0, 0, axis_index_groups=same_core, tiled=True
    )
    key_grad, value_grad, attended = pl.pallas_call(
        key_grad_kernel,
        out_shape=(shape((rows, cols)),) * 3,
        in_specs=[SMEM] * 3 + [VMEM] * 2 + [ANY] * 16,
        out_specs=(VMEM,) * 3,
        scratch_shapes=[
            pltpu.VMEM((halo, cols), jnp.bfloat16),
            pltpu.VMEM((halo + 5 * STAT_ROWS, cols), jnp.bfloat16),
            pltpu.VMEM((halo // BLK, 2 * heads, BLK), f32),
            head_sums,
            head_sums,
            pltpu.SMEM((rows // BLK, halo // BLK), jnp.int32),
            pltpu.SMEM((rows // BLK,), jnp.int32),
            pltpu.VMEM((rows, cols), f32),
            pltpu.VMEM((ranks - 1, rows, cols), jnp.bfloat16),
            pltpu.SemaphoreType.DMA((14,)),
        ],
        compiler_params=LARGE,
        cost_estimate=cost(10),
        name="key_grad",
    )(*tables, key_heads, value_heads, *queries, *grads, own_out, *parts)

    weight_grad = pl.pallas_call(
        last_sum_kernel,
        out_shape=shape(blocks.shape[1:], f32),
        in_specs=[VMEM],
        out_specs=VMEM,
        compiler_params=PARAMS,
        cost_estimate=cost(1),
        name="last_sum",
    )(after(spread, key_grad)).T
    return (attended, query_grad, key_grad, value_grad, weight_grad)


def solution(mesh):
    in_specs = (
        P("seq", "tp"),
        P("seq", "tp"),
        P("seq", "tp"),
        P("tp", None),
        P("seq", "tp"),
        P("seq"),
        P(),
        P(),
    )
    out_specs = (P("seq", "tp"), P("seq", "tp"), P("seq", "tp"), P("seq", "tp"), P("tp", "seq"))
    return jax.shard_map(local, mesh=mesh, in_specs=in_specs, out_specs=out_specs, check_vma=False)
```

```python
import math

import jax
import jax.numpy as jnp
from jax import lax
from jax.experimental import pallas as pl
from jax.experimental.pallas import tpu as pltpu
from jax.sharding import PartitionSpec as P

HD = 128
BLK = 256
WINDOW = 4
SCALE = 1.0 / math.sqrt(HD)
TWO = SCALE * math.log2(math.e)
STAT_ROWS = 32
CHUNK = 4
SHIFTS = (0, 3, 1, 2, 2)

NT = (((1,), (1,)), ((), ()))
NN = (((1,), (0,)), ((), ()))
TN = (((0,), (0,)), ((), ()))


def mm(a, b, dims):
    return lax.dot_general(a, b, dims, preferred_element_type=jnp.float32)


def shifted(value, steps):
    count = lax.axis_size("seq")
    return lax.ppermute(value, "seq", [(i, (i + steps) % count) for i in range(count)])


def swapped(value):
    return lax.ppermute(value, "seq", [(i, i ^ 1) for i in range(lax.axis_size("seq"))])


def along_tp(value, steps):
    count = lax.axis_size("tp")
    return lax.ppermute(value, "tp", [(i, (i + steps) % count) for i in range(count)])


def relayed(from_left, from_right):
    return swapped(from_left), swapped(from_right)


def start_halo(core, refs, buf, sems, first, with_own):
    own, mate, left, right, to_even, to_odd = refs
    rows = left.shape[0]

    def slot(index):
        return buf.at[pl.ds(pl.multiple_of(index * rows, 32), rows)]

    copies = [
        pltpu.make_async_copy(left, slot(0), sems.at[first]),
        pltpu.make_async_copy(right, slot(4), sems.at[first + 1]),
        pltpu.make_async_copy(mate, slot(3 - 2 * core), sems.at[first + 2]),
    ]
    if with_own:
        copies.append(pltpu.make_async_copy(own, slot(2), sems.at[first + 3]))
    for copy in copies:
        copy.start()
    even = pltpu.make_async_copy(to_even, slot(1), sems.at[first + 4])
    odd = pltpu.make_async_copy(to_odd, slot(3), sems.at[first + 4])

    @pl.when(core == 0)
    def _():
        even.start()

    @pl.when(core != 0)
    def _():
        odd.start()

    return copies + [even]


def in_chunks(count, body):
    def whole(c, carry):
        body(c * CHUNK, CHUNK)
        return carry

    lax.fori_loop(0, count // CHUNK, whole, 0)
    rest = count % CHUNK
    for size in range(1, CHUNK):

        @pl.when(rest == size)
        def _():
            body(count - size, size)


def stacked(ref, rows, col):
    return jnp.concatenate([ref[pl.ds(row, BLK), col] for row in rows], axis=0)


def folded(x, op):
    total = x[:, :HD]
    for i in range(1, x.shape[1] // HD):
        total = op(total, x[:, i * HD : (i + 1) * HD])
    return total


def forward_kernel(pos_ref, pat_ref, cnt_ref, q_ref, mask_ref, weight_hbm, *rest):
    pieces, rest = rest[:5], rest[5:]
    k_refs, v_refs = rest[:6], rest[6:12]
    outs, rest = rest[12:19], rest[19:]
    sent_ref, mine_ref, theirs_ref, own_ref, *sends = rest[:7]
    out_ref, masked_ref, kbuf, vbuf, wbuf, cbuf, top, total, acc, stats, sems = rest[7:]
    leaving = []

    def leave(buf):
        n = len(leaving)
        leaving.append(pltpu.make_async_copy(buf, outs[n], sems.at[16 + n]))
        leaving[-1].start()

    pos = pos_ref[0]
    core = pos % 2
    rows, cols = q_ref.shape
    heads, blocks = cols // HD, rows // BLK
    waits = start_halo(core, k_refs, kbuf, sems, 0, True)
    waits += start_halo(core, v_refs, vbuf, sems, 5, True)
    ranks = wbuf.shape[1] // cols
    later = [pltpu.make_async_copy(weight_hbm, wbuf, sems.at[10])]
    for x, (piece, shift) in enumerate(zip(pieces, SHIFTS)):
        low = 0 if x < ranks else rows - piece.shape[0]
        place = cbuf.at[
            pl.ds(low, piece.shape[0]),
            pl.ds(pl.multiple_of((pos_ref[1] + shift) % ranks * cols, HD), cols),
        ]
        later.append(pltpu.make_async_copy(piece, place, sems.at[11 + x]))
    for copy in waits:
        copy.wait()
    for copy in later:
        copy.start()
    for i in range(blocks):
        block = pos * blocks + i
        tok = slice(i * BLK, (i + 1) * BLK)
        top[...] = jnp.full_like(top, -1e30)
        total[...] = jnp.zeros_like(total)
        acc[...] = jnp.zeros_like(acc)

        def body(first, size):
            places = [
                pl.multiple_of((pat_ref[first + c, block] - pos * blocks + WINDOW) * BLK, BLK)
                for c in range(size)
            ]
            for h in range(heads):
                col = slice(h * HD, (h + 1) * HD)
                s = mm(q_ref[tok, col], stacked(kbuf, places, col), NT)
                high = jnp.max(folded(s, jnp.maximum), axis=1, keepdims=True) * TWO
                old = top[h]
                new = jnp.maximum(old, high)
                p = jnp.exp2(s * TWO - jnp.concatenate([new] * (2 * size), 1))
                fade = jnp.exp2(old - new)
                top[h] = new
                total[h] = total[h] * fade + folded(p, jnp.add)
                acc[h] = acc[h] * fade + mm(
                    p.astype(jnp.bfloat16), stacked(vbuf, places, col), NN
                )

        in_chunks(cnt_ref[block], body)
        for h in range(heads):
            col = slice(h * HD, (h + 1) * HD)
            whole = jnp.sum(total[h], axis=1, keepdims=True)
            out = acc[h] * (1.0 / whole)
            rounded = out.astype(jnp.bfloat16)
            out_ref[tok, col] = rounded
            lse = top[h] + jnp.log(whole) * math.log2(math.e)
            stats[h : h + 1, tok] = lse.T[0:1]
    for copy in later:
        copy.wait()
    kept = jnp.broadcast_to(mask_ref[...], (HD, rows)).astype(jnp.float32).T == 1.0
    half = cols // 2
    for part in range(2):
        grad = mm(cbuf[...], wbuf[part * half : (part + 1) * half, :], NT)
        for h in range(half // HD):
            head = part * (half // HD) + h
            col = slice(head * HD, (head + 1) * HD)
            one = jnp.where(kept, grad[:, h * HD : (h + 1) * HD], 0.0).astype(jnp.bfloat16)
            sent_ref[0:rows, col] = one
            masked_ref[:, col] = jnp.where(kept, out_ref[:, col].astype(jnp.float32), 0.0).astype(
                jnp.bfloat16
            )
            dots = one.astype(jnp.float32) * out_ref[:, col].astype(jnp.float32)
            stats[heads + head : heads + head + 1, :] = jnp.sum(dots.T, axis=0, keepdims=True)
    whole = stats[...]
    high = whole.astype(jnp.bfloat16).astype(jnp.float32)
    middle = (whole - high).astype(jnp.bfloat16).astype(jnp.float32)
    low = whole - high - middle
    parts = jnp.concatenate([high, middle, low, jnp.zeros_like(low)], axis=0)
    sent_ref[rows : rows + STAT_ROWS, :] = parts.astype(jnp.bfloat16)
    leave(sent_ref)
    narrow = mine_ref.shape[1]
    count = mine_ref.shape[0] // ranks
    for j in range(ranks):
        part = mm(cbuf[:, j * cols : (j + 1) * cols], masked_ref[...], TN).astype(jnp.bfloat16)
        for x in range(count):
            low = part[2 * x * narrow : (2 * x + 1) * narrow]
            high = part[(2 * x + 1) * narrow : (2 * x + 2) * narrow]
            mine_ref[j * count + x] = jnp.where(core == 0, low, high)
            theirs_ref[j * count + x] = jnp.where(core == 0, high, low)
    leave(mine_ref)
    leave(theirs_ref)
    for shift in range(ranks):
        first = pl.multiple_of((pos_ref[1] + shift) % ranks * cols, HD)
        part = mm(out_ref[...], wbuf[:, pl.ds(first, cols)], NN)
        ref = sends[shift - 1] if shift else own_ref
        ref[...] = part.astype(ref.dtype)
        leave(ref)
    for copy in leaving:
        copy.wait()


def chip_sum_kernel(mine_ref, arrived_ref, out_ref):
    total = mine_ref[...].astype(jnp.float32) + arrived_ref[...].astype(jnp.float32)
    out_ref[...] = total.astype(out_ref.dtype)


def last_sum_kernel(in_ref, out_ref):
    total = in_ref[0].astype(jnp.float32)
    for i in range(1, in_ref.shape[0]):
        total += in_ref[i].astype(jnp.float32)
    out_ref[...] = total


def joined_stats(parts):
    parts = parts.astype(jnp.float32)
    return parts[0:8] + parts[8:16] + parts[16:24]


def query_grad_kernel(pos_ref, pat_ref, cnt_ref, q_hbm, g_hbm, *rest):
    k_refs, v_refs = rest[:6], rest[6:12]
    dq_ref, q_ref, g_ref, kbuf, vbuf, acc, sems = rest[12:]
    pos = pos_ref[0]
    core = pos % 2
    rows, cols = q_ref.shape
    heads, blocks = cols // HD, rows // BLK
    waits = start_halo(core, k_refs, kbuf, sems, 0, True)
    waits += start_halo(core, v_refs, vbuf, sems, 5, True)
    for x, (src, dst) in enumerate(((q_hbm, q_ref), (g_hbm, g_ref))):
        waits.append(pltpu.make_async_copy(src, dst, sems.at[10 + x]))
        waits[-1].start()
    for copy in waits:
        copy.wait()
    stats = joined_stats(g_ref[rows : rows + STAT_ROWS, :])
    for i in range(blocks):
        block = pos * blocks + i
        tok = slice(i * BLK, (i + 1) * BLK)
        turned = [
            jnp.broadcast_to(stats[x : x + 1, tok], (HD, BLK)).T for x in range(2 * heads)
        ]
        acc[...] = jnp.zeros_like(acc)

        def body(first, size):
            places = [
                pl.multiple_of((pat_ref[first + c, block] - pos * blocks + WINDOW) * BLK, BLK)
                for c in range(size)
            ]
            for h in range(heads):
                col = slice(h * HD, (h + 1) * HD)
                k = stacked(kbuf, places, col)
                s = mm(q_ref[tok, col], k, NT)
                p = jnp.exp2(s * TWO - jnp.concatenate([turned[h]] * (2 * size), 1))
                dp = mm(g_ref[tok, col], stacked(vbuf, places, col), NT)
                ds = p * (dp - jnp.concatenate([turned[heads + h]] * (2 * size), 1))
                acc[h] += mm(ds.astype(jnp.bfloat16), k, NN)

        in_chunks(cnt_ref[block], body)
        for h in range(heads):
            dq_ref[tok, h * HD : (h + 1) * HD] = (acc[h] * SCALE).astype(jnp.bfloat16)


def key_grad_kernel(pos_ref, pat_ref, cnt_ref, k_hbm, v_hbm, *rest):
    q_refs, g_refs, parts, rest = rest[:6], rest[6:12], rest[12:16], rest[16:]
    dk_ref, dv_ref, attended_ref, qbuf, gbuf, stats, dk, dv = rest[:8]
    lists, sizes, own_part, more, k_ref, v_ref, sems = rest[8:]
    pos = pos_ref[0]
    core = pos % 2
    rows, cols = k_ref.shape
    heads, blocks = cols // HD, rows // BLK
    all_blocks = pat_ref.shape[1]
    sent_rows = rows + STAT_ROWS
    waits = start_halo(core, q_refs, qbuf, sems, 0, True)
    waits += start_halo(core, g_refs, gbuf, sems, 5, True)
    for x, (src, dst) in enumerate(((k_hbm, k_ref), (v_hbm, v_ref))):
        waits.append(pltpu.make_async_copy(src, dst, sems.at[14 + x]))
        waits[-1].start()
    for i in range(blocks):
        sizes[i] = 0

    def from_block(near, carry):
        block = pos * blocks - WINDOW + near
        inside = (block >= 0) & (block < all_blocks)
        block = jnp.clip(block, 0, all_blocks - 1)

        def slot(j, inner):
            place = pat_ref[j, block] - pos * blocks

            @pl.when((place >= 0) & (place < blocks))
            def _():
                size = sizes[place]
                lists[place, size] = near
                sizes[place] = size + 1

            return inner

        lax.fori_loop(0, jnp.where(inside, cnt_ref[block], 0), slot, 0)
        return carry

    lax.fori_loop(0, 2 * WINDOW + blocks, from_block, 0)
    for copy in waits:
        copy.wait()
    later = [pltpu.make_async_copy(parts[0], own_part, sems.at[10])]
    for x, part in enumerate(parts[1:]):
        later.append(pltpu.make_async_copy(part, more.at[x], sems.at[11 + x]))
    for copy in later:
        copy.start()
    for device in range(gbuf.shape[0] // sent_rows):
        first = device * sent_rows + rows
        both = joined_stats(gbuf[first : first + STAT_ROWS, :])
        for part in range(blocks):
            stats[device * blocks + part] = both[:, part * BLK : (part + 1) * BLK]
    for i in range(blocks):
        own = slice(i * BLK, (i + 1) * BLK)
        dk[...] = jnp.zeros_like(dk)
        dv[...] = jnp.zeros_like(dv)

        def body(first, size):
            nears = [lists[i, first + c] for c in range(size)]
            q_rows = [pl.multiple_of(near * BLK, BLK) for near in nears]
            g_rows = [
                pl.multiple_of(near // blocks * sent_rows + near % blocks * BLK, 32)
                for near in nears
            ]
            both = jnp.concatenate([stats[near] for near in nears], axis=1)
            for h in range(heads):
                col = slice(h * HD, (h + 1) * HD)
                q = stacked(qbuf, q_rows, col)
                g = stacked(gbuf, g_rows, col)
                s = mm(k_ref[own, col], q, NT)
                p = jnp.exp2(s * TWO - both[h : h + 1])
                dp = mm(v_ref[own, col], g, NT)
                ds = p * (dp - both[heads + h : heads + h + 1])
                dv[h] += mm(p.astype(jnp.bfloat16), g, NN)
                dk[h] += mm(ds.astype(jnp.bfloat16), q, NN)

        in_chunks(sizes[i], body)
        for h in range(heads):
            col = slice(h * HD, (h + 1) * HD)
            dk_ref[own, col] = (dk[h] * SCALE).astype(jnp.bfloat16)
            dv_ref[own, col] = dv[h].astype(jnp.bfloat16)
    for copy in later:
        copy.wait()
    whole = own_part[...]
    for x in range(more.shape[0]):
        whole += more[x].astype(jnp.float32)
    attended_ref[...] = whole.astype(jnp.bfloat16)


SMEM = pl.BlockSpec(memory_space=pltpu.SMEM)
VMEM = pl.BlockSpec(memory_space=pltpu.VMEM)
ANY = pl.BlockSpec(memory_space=pltpu.HBM)
PARAMS = pltpu.CompilerParams(vmem_limit_bytes=24 * 1024 * 1024)
LARGE = pltpu.CompilerParams(vmem_limit_bytes=60 * 1024 * 1024)


def shape(dims, dtype=jnp.bfloat16):
    return jax.ShapeDtypeStruct(dims, dtype)


def cost(micros):
    return pl.CostEstimate(flops=int(micros * 1.1e8), bytes_accessed=1024, transcendentals=0)


def after(value, *others):
    return lax.optimization_barrier((value,) + others)[0]


def local(
    query_heads,
    key_heads,
    value_heads,
    out_weight,
    cotangent,
    loss_mask,
    block_pattern,
    block_counts,
):
    rows, cols = query_heads.shape
    heads = cols // HD
    width = out_weight.shape[1]
    ranks = lax.axis_size("tp")
    chips = lax.axis_size("seq") // 2
    position = lax.axis_index("seq")
    where = jnp.stack([position, lax.axis_index("tp")]).astype(jnp.int32)
    tables = (where, block_pattern.T, block_counts)
    f32 = jnp.float32

    key_mate, value_mate, query_mate = (swapped(x) for x in (key_heads, value_heads, query_heads))
    key_left, key_right = shifted(key_heads, 2), shifted(key_heads, -2)
    value_after = after(value_heads, key_left, key_right)
    value_left, value_right = shifted(value_after, 2), shifted(value_after, -2)
    cot_prev, cot_next = along_tp(cotangent, 1), along_tp(cotangent, -1)
    cots = (cotangent, cot_prev, cot_next)
    cots += (along_tp(cot_next[: rows // 2], -1), along_tp(cot_prev[rows // 2 :], 1))
    keys = (key_heads, key_mate, key_left, key_right) + relayed(key_left, key_right)
    query_after = after(query_heads, value_left, value_right)
    query_left, query_right = shifted(query_after, 2), shifted(query_after, -2)
    queries = (query_heads, query_mate, query_left, query_right) + relayed(query_left, query_right)

    values = (value_heads, value_mate, value_left, value_right) + relayed(value_left, value_right)

    halo = 5 * rows
    sent_shape = shape((rows + STAT_ROWS, cols))
    head_sums = pltpu.VMEM((heads, BLK, HD), f32)
    blocks = shape((chips, width // chips // 2, cols))
    made = (sent_shape, blocks, blocks, shape((rows, cols), f32)) + (shape((rows, cols)),) * 3
    sent, mine, theirs, own_out, *sends = pl.pallas_call(
        forward_kernel,
        out_shape=made,
        in_specs=[SMEM] * 3 + [VMEM] * 2 + [ANY] * 18,
        out_specs=(ANY,) * 7,
        scratch_shapes=[pltpu.VMEM(x.shape, x.dtype) for x in made]
        + [
            pltpu.VMEM((rows, cols), jnp.bfloat16),
            pltpu.VMEM((rows, cols), jnp.bfloat16),
            pltpu.VMEM((halo, cols), jnp.bfloat16),
            pltpu.VMEM((halo, cols), jnp.bfloat16),
            pltpu.VMEM((cols, width), jnp.bfloat16),
            pltpu.VMEM((rows, width), jnp.bfloat16),
            head_sums,
            head_sums,
            head_sums,
            pltpu.VMEM((2 * heads, rows), f32),
            pltpu.SemaphoreType.DMA((23,)),
        ],
        compiler_params=LARGE,
        cost_estimate=cost(10),
        name="attention_forward",
    )(*tables, query_heads, loss_mask.reshape(1, rows), out_weight, *cots, *keys, *values)
    sent_mate = swapped(sent)
    sent_left, sent_right = shifted(sent, 2), shifted(sent, -2)
    arrived = swapped(after(theirs, query_left, query_right))
    parts = [along_tp(send, step + 1) for step, send in enumerate(sends)]

    some = pl.BlockSpec((chips // 4,) + blocks.shape[1:], lambda i: (i, 0, 0))
    chip_sum = pl.pallas_call(
        chip_sum_kernel,
        grid=(4,),
        out_shape=blocks,
        in_specs=[some, some],
        out_specs=some,
        compiler_params=PARAMS,
        cost_estimate=cost(1),
        name="chip_sum",
    )(mine, arrived)

    query_grad = pl.pallas_call(
        query_grad_kernel,
        out_shape=shape((rows, cols)),
        in_specs=[SMEM] * 3 + [ANY] * 14,
        out_specs=VMEM,
        scratch_shapes=[
            pltpu.VMEM((rows, cols), jnp.bfloat16),
            pltpu.VMEM((rows + STAT_ROWS, cols), jnp.bfloat16),
            pltpu.VMEM((halo, cols), jnp.bfloat16),
            pltpu.VMEM((halo, cols), jnp.bfloat16),
            head_sums,
            pltpu.SemaphoreType.DMA((12,)),
        ],
        compiler_params=LARGE,
        cost_estimate=cost(10),
        name="query_grad",
    )(*tables, after(query_heads, chip_sum), sent, *keys, *values)
    grads = (sent, sent_mate, sent_left, sent_right) + relayed(sent_left, sent_right)

    same_core = [[2 * i + c for i in range(chips)] for c in range(2)]
    spread = lax.all_to_all(
        after(chip_sum, query_grad), "seq", 0, 0, axis_index_groups=same_core, tiled=True
    )
    key_grad, value_grad, attended = pl.pallas_call(
        key_grad_kernel,
        out_shape=(shape((rows, cols)),) * 3,
        in_specs=[SMEM] * 3 + [ANY] * 18,
        out_specs=(VMEM,) * 3,
        scratch_shapes=[
            pltpu.VMEM((halo, cols), jnp.bfloat16),
            pltpu.VMEM((halo + 5 * STAT_ROWS, cols), jnp.bfloat16),
            pltpu.VMEM((halo // BLK, 2 * heads, BLK), f32),
            head_sums,
            head_sums,
            pltpu.SMEM((rows // BLK, halo // BLK), jnp.int32),
            pltpu.SMEM((rows // BLK,), jnp.int32),
            pltpu.VMEM((rows, cols), f32),
            pltpu.VMEM((ranks - 1, rows, cols), jnp.bfloat16),
            pltpu.VMEM((rows, cols), jnp.bfloat16),
            pltpu.VMEM((rows, cols), jnp.bfloat16),
            pltpu.SemaphoreType.DMA((16,)),
        ],
        compiler_params=LARGE,
        cost_estimate=cost(10),
        name="key_grad",
    )(*tables, key_heads, value_heads, *queries, *grads, own_out, *parts)

    weight_grad = pl.pallas_call(
        last_sum_kernel,
        out_shape=shape(blocks.shape[1:], f32),
        in_specs=[VMEM],
        out_specs=VMEM,
        compiler_params=PARAMS,
        cost_estimate=cost(1),
        name="last_sum",
    )(after(spread, key_grad)).T
    return (attended, query_grad, key_grad, value_grad, weight_grad)


def solution(mesh):
    in_specs = (
        P("seq", "tp"),
        P("seq", "tp"),
        P("seq", "tp"),
        P("tp", None),
        P("seq", "tp"),
        P("seq"),
        P(),
        P(),
    )
    out_specs = (P("seq", "tp"), P("seq", "tp"), P("seq", "tp"), P("seq", "tp"), P("tp", "seq"))
    return jax.shard_map(local, mesh=mesh, in_specs=in_specs, out_specs=out_specs, check_vma=False)
```
